128 devices in a mesh: blk: 32 (over x, y, core), cross: 4 (over z).
Axes of the slice: x: 4, y: 4, z: 4, core: 2. Of those that a mesh axis runs over, the one named last changes fastest.
Arguments:
- base_column: int32 [32768], P(('blk', 'cross')), may hold values from 0 to 511
- base_zbin: int32 [32768, 128], P(('blk', 'cross')), may hold values from 0 to 1023
- base_frac: float32 [3, 32768, 128], P(None, ('blk', 'cross')), may hold values from 0 to 1
- base_weight: float32 [32768, 128], P(('blk', 'cross')), may hold values from 0.25 to 4
- fine_column: int32 [114688], P(('blk', 'cross')), may hold values from 0 to 224
- fine_zbin: int32 [114688, 128], P(('blk', 'cross')), may hold values from 0 to 62
- fine_frac: float32 [3, 114688, 128], P(None, ('blk', 'cross')), may hold values from 0 to 1
- fine_weight: float32 [114688, 128], P(('blk', 'cross')), may hold values from 0.25 to 4
- tile_box: int32 [114688], P(('blk', 'cross')), may hold values from 0 to 1023, as said below
- box_home: int32 [1024], replicated, may hold values from 0 to 127, as said below
- box_anchor: int32 [1024], replicated, may hold values from 0 to 255, as said below
Outputs:
- base_mass: float32 [256, 256, 1024], P('blk', 'cross')
- fine_mass: float32 [1024, 16384], P(('blk', 'cross'))
The draws below stay inside these ranges and needn't reach their ends.
Inputs may be any that keep to these rules, and one draw needn't show every extreme that they name: `box_home`: box r is owned by device r // 8; every device is home to exactly 8 boxes, and the 8 boxes of one owner have distinct homes. `box_anchor`: boxes with the same home have distinct positions. `tile_box`: the tiles of one device are sorted by the owner of their box; every device holds 16 tiles of the boxes of each owner of a quarter of the owners, and 4 of each of the others.
All inputs are finite; a program needn't handle non-finite values.
Results may differ from the reference program's by a relative error of at most 0.0003.
Values sent between devices are 32-bit elements; how exact they have to be, the bound alone decides.
No kernel may reach another device: no remote copies, remote signals or barrier semaphores. Data moves between devices by JAX's collectives and lax.ppermute only.
A program may use at most 192 MiB of HBM per device.

```python
import math
import jax
import jax.numpy as jnp
from jax import lax

CX = 8
CY = 64
NZ = 1024
BT = 256
PT = 128
BX = 8
BY = 8
BZ = 32
BPH = 8
CAP = 16
LOW = 4
NODES = 128
NX = 256
NY = 256
LATTICE = 256
NBOX = 1024
FT = 896
NBT = 32768
NFT = 114688


def box_tables(key):
    first_perm = jax.random.permutation(jax.random.fold_in(key, 201), NODES).astype(jnp.int32)
    second_perm = jax.random.permutation(jax.random.fold_in(key, 202), NODES).astype(jnp.int32)
    shifts = jax.random.permutation(jax.random.fold_in(key, 203), NODES)[:BPH].astype(jnp.int32)
    homes = first_perm[(second_perm[:, None] + shifts[None, :]) % NODES]
    keys = jax.random.split(jax.random.fold_in(key, 204), NODES)

    def one_home(single):
        inner = jax.random.permutation(jax.random.fold_in(single, 5), LATTICE - 2)[:BPH - 2].astype(jnp.int32) + 1
        chosen = jnp.concatenate([inner, jnp.array([0, LATTICE - 1], jnp.int32)])
        order = jax.random.permutation(jax.random.fold_in(single, 6), BPH)
        return chosen[order].astype(jnp.int32)
    positions = jax.vmap(one_home)(keys)
    anchors = positions[homes, jnp.arange(BPH, dtype=jnp.int32)[None, :]]
    return (homes.astype(jnp.int32), anchors.astype(jnp.int32))


def draw_box_home(key, part):
    homes, anchors = box_tables(key)
    return homes.reshape(-1)


def draw_box_anchor(key, part):
    homes, anchors = box_tables(key)
    return anchors.reshape(-1)


def draw_tile_box(key, part):
    key = jax.random.fold_in(key, 2)
    heavy = jax.random.permutation(jax.random.fold_in(key, 1), NODES) < NODES // 4
    loads = jnp.where(heavy, CAP, LOW).astype(jnp.int32)
    owners = jnp.repeat(jnp.arange(NODES, dtype=jnp.int32), loads, total_repeat_length=FT)
    keys = jax.random.split(jax.random.fold_in(key, 3), NODES)

    def one_home(single):
        local = jax.random.randint(single, (FT,), 0, BPH).astype(jnp.int32)
        local = local.at[0].set(0).at[FT - 1].set(BPH - 1)
        return owners * BPH + local
    return jax.vmap(one_home)(keys).reshape(-1).astype(jnp.int32)


def set_ends(entries, key, least, top_value):
    place = [jax.random.randint(jax.random.fold_in(key, axis), (), 0, length) for axis, length in enumerate(entries.shape)]
    main_axis = entries.shape.index(max(entries.shape))
    neighbour = place[:main_axis] + [(place[main_axis] + 1) % entries.shape[main_axis]] + place[main_axis + 1:]
    return entries.at[tuple(place)].set(least).at[tuple(neighbour)].set(top_value)


def levels(stream_key, shape, shards, smallest, top_value):
    def one(dim, blocks):
        heights = jax.random.uniform(jax.random.fold_in(jax.random.fold_in(stream_key, 6), dim), (blocks,), jnp.float32, smallest / len(shards), top_value / len(shards))
        return jnp.repeat(jnp.exp(heights), shape[dim] // blocks).reshape((-1,) + (1,) * (len(shape) - dim - 1))

    factor_of = one(*shards[0])
    for cut in shards[1:]:
        factor_of = factor_of * one(*cut)
    return factor_of


def setup_inputs(seed: int = 0) -> dict:
    arg_keys = jax.random.split(jax.random.key(seed), 12)
    base_column = set_ends(jax.random.randint(arg_keys[0], (NBT,), 0, CX * CY), jax.random.fold_in(arg_keys[0], 1), 0, (CX * CY) - 1).astype(jnp.int32)
    base_zbin = set_ends(jax.random.randint(arg_keys[1], (NBT, PT), 0, NZ), jax.random.fold_in(arg_keys[1], 1), 0, NZ - 1).astype(jnp.int32)
    base_frac = jnp.clip(1.0 * jax.random.uniform(arg_keys[2], (3, NBT, PT), jnp.float32) ** levels(arg_keys[2], (3, NBT, PT), ((1, 128),), -0.2, 0.2), 0.0, 1.0)
    base_weight = jnp.clip(jnp.exp(math.log(4.0) - 2.7725887 * jax.random.uniform(arg_keys[3], (NBT, PT), jnp.float32) ** levels(arg_keys[3], (NBT, PT), ((0, 128),), -0.2, 0.2)), 0.25, 4.0)
    fine_column = set_ends(jax.random.randint(arg_keys[4], (NFT,), 0, (2 * BX - 1) * (2 * BY - 1)), jax.random.fold_in(arg_keys[4], 1), 0, ((2 * BX - 1) * (2 * BY - 1)) - 1).astype(jnp.int32)
    fine_zbin = set_ends(jax.random.randint(arg_keys[5], (NFT, PT), 0, 2 * BZ - 1), jax.random.fold_in(arg_keys[5], 1), 0, (2 * BZ - 1) - 1).astype(jnp.int32)
    fine_frac = jnp.clip(1.0 * jax.random.uniform(arg_keys[6], (3, NFT, PT), jnp.float32) ** levels(arg_keys[6], (3, NFT, PT), ((1, 128),), -0.2, 0.2), 0.0, 1.0)
    fine_weight = jnp.clip(jnp.exp(math.log(4.0) - 2.7725887 * jax.random.uniform(arg_keys[7], (NFT, PT), jnp.float32) ** levels(arg_keys[7], (NFT, PT), ((0, 128),), -0.2, 0.2)), 0.25, 4.0)
    tile_box = draw_tile_box(jax.random.fold_in(arg_keys[11], 71), 0)
    box_home = draw_box_home(jax.random.fold_in(arg_keys[11], 71), 0)
    box_anchor = draw_box_anchor(jax.random.fold_in(arg_keys[11], 71), 0)
    return dict(base_column=base_column, base_zbin=base_zbin, base_frac=base_frac, base_weight=base_weight, fine_column=fine_column, fine_zbin=fine_zbin, fine_frac=fine_frac, fine_weight=fine_weight, tile_box=tile_box, box_home=box_home, box_anchor=box_anchor)


def corner_list(fractions, masses):
    along_x, along_y, along_z = fractions[0], fractions[1], fractions[2]
    result = []
    for first in (0, 1):
        for second in (0, 1):
            for third in (0, 1):
                part_x = along_x if first else 1.0 - along_x
                part_y = along_y if second else 1.0 - along_y
                part_z = along_z if third else 1.0 - along_z
                result.append((first, second, third, masses * part_x * part_y * part_z))
    return result


def reference(base_column, base_zbin, base_frac, base_weight, fine_column, fine_zbin, fine_frac, fine_weight, tile_box, box_home, box_anchor):
    n_cross = NY // CY
    n_blk = NX // CX
    total_cells = NX * NY * NZ

    def base_home(total, home):
        start = (home * BT).astype(jnp.int32)
        columns = lax.dynamic_slice_in_dim(base_column, start, BT, 0)
        zbins = lax.dynamic_slice_in_dim(base_zbin, start, BT, 0)
        fractions = lax.dynamic_slice_in_dim(base_frac, start, BT, 1)
        masses = lax.dynamic_slice_in_dim(base_weight, start, BT, 0)
        place_x = (home // n_cross) * CX + columns // CY
        place_y = (home % n_cross) * CY + columns % CY
        values = []
        indices = []
        for first, second, third, weight in corner_list(fractions, masses):
            cell_x = ((place_x + first) % NX)[:, None]
            cell_y = ((place_y + second) % NY)[:, None]
            cell_z = (zbins + third) % NZ
            indices.append(((cell_x * NY + cell_y) * NZ + cell_z).reshape(-1).astype(jnp.int32))
            values.append(weight.reshape(-1))
        added = jax.ops.segment_sum(jnp.concatenate(values), jnp.concatenate(indices), num_segments=total_cells)
        return total + added, 0

    deposit, _ = lax.scan(base_home, jnp.zeros((total_cells,), jnp.float32), jnp.arange(NODES, dtype=jnp.int32))

    fine_columns = 4 * BX * BY
    stride = 2 * BY - 1
    fine_cells = NBOX * fine_columns * 2 * BZ

    def fine_home(total, home):
        start = (home * FT).astype(jnp.int32)
        boxes = lax.dynamic_slice_in_dim(tile_box, start, FT, 0)
        columns = lax.dynamic_slice_in_dim(fine_column, start, FT, 0)
        zbins = lax.dynamic_slice_in_dim(fine_zbin, start, FT, 0)
        fractions = lax.dynamic_slice_in_dim(fine_frac, start, FT, 1)
        masses = lax.dynamic_slice_in_dim(fine_weight, start, FT, 0)
        place_x = columns // stride
        place_y = columns % stride
        values = []
        indices = []
        for first, second, third, weight in corner_list(fractions, masses):
            target = (place_x + first) * (2 * BY) + place_y + second
            flat = ((boxes * fine_columns + target)[:, None] * (2 * BZ)) + zbins + third
            indices.append(flat.reshape(-1).astype(jnp.int32))
            values.append(weight.reshape(-1))
        added = jax.ops.segment_sum(jnp.concatenate(values), jnp.concatenate(indices), num_segments=fine_cells)
        return total + added, 0

    fine_flat, _ = lax.scan(fine_home, jnp.zeros((fine_cells,), jnp.float32), jnp.arange(NODES, dtype=jnp.int32))
    fine_mass = fine_flat.reshape(NBOX, fine_columns * 2 * BZ)

    restricted = fine_mass.reshape(NBOX, BX, 2, BY, 2, BZ, 2).sum(axis=(2, 4, 6)).reshape(NBOX, BX * BY * BZ)
    lattice = deposit.reshape(n_blk, CX // BX, BX, n_cross, CY // BY, BY, NZ // BZ, BZ)
    lattice = lattice.transpose(0, 3, 1, 4, 6, 2, 5, 7).reshape(NODES, LATTICE, BX * BY * BZ)
    lattice = lattice.at[box_home, box_anchor].add(restricted)
    base_mass = lattice.reshape(n_blk, n_cross, CX // BX, CY // BY, NZ // BZ, BX, BY, BZ)
    base_mass = base_mass.transpose(0, 2, 5, 1, 3, 6, 4, 7).reshape(NX, NY, NZ)
    return base_mass, fine_mass
```

```python
import jax
import jax.numpy as jnp
from jax import lax
from jax.experimental import pallas as pl
from jax.experimental.pallas import tpu as pltpu
from jax.sharding import PartitionSpec as P

CX = 8
CY = 64
NZ = 1024
BPH = 8
NODES = 128
PT = 128
BT = 256
FT = 896
GROUPS = FT // 4
SLOTS = 4
GX = CX + 1
GY = CY + 1
AXES = ("blk", "cross")
PARTS = 4
LINE = SLOTS * 1024 + 128
VMEM_BYTES = 62 * 1024 * 1024
f32 = jnp.float32
bf16 = jnp.bfloat16
i32 = jnp.int32


def shifted(value, axis, steps):
    count = lax.axis_size(axis)
    pairs = [(source, (source + steps) % count) for source in range(count)]
    return lax.ppermute(value, axis, pairs)


def diagonal(value):
    blocks, columns = lax.axis_size("blk"), lax.axis_size("cross")
    pairs = [
        (b * columns + c, (b + 1) % blocks * columns + (c + 1) % columns)
        for b in range(blocks)
        for c in range(columns)
    ]
    return lax.ppermute(value, AXES, pairs)


def iota(shape, dim):
    return lax.broadcasted_iota(i32, shape, dim)


def two_terms(value):
    high = value.astype(bf16).astype(f32)
    return high, value - high


def nt_dot(left, right):
    return lax.dot_general(left, right, (((1,), (1,)), ((), ())), preferred_element_type=f32)


def corner_weights(u, v, w, m):
    result = []
    for part_x in (1.0 - u, u):
        row = []
        for part_y in (1.0 - v, v):
            plane = m * part_x * part_y
            row.append((plane * (1.0 - w), plane * w))
        result.append(row)
    return result


def fine_profile_kernel(
    box_ref, boxes_ref, columns_ref, zbin_ref, frac_ref, mass_ref, out_ref, label_ref, head_ref, last_ref
):
    part = pl.program_id(0)

    @pl.when(part == 0)
    def _():
        out_ref[...] = jnp.zeros(out_ref.shape, f32)
        boxes = boxes_ref[...]
        columns = columns_ref[...]
        x = (columns * 4370) >> 16
        y = columns - x * 15
        label_ref[...] = ((y & 1) * 1024 + (x * 8 + (y >> 1)) * 8 + (boxes & 7)).astype(f32)
        head_ref[...] = jnp.zeros((1, 128), f32)
        last_ref[0] = -1

    four_lanes = iota((1, 128), 1) // 4
    sub = iota((8, PT), 0)
    four = sub % 4
    turn = (iota((8, PT), 1) // 32 - four) & 3
    z_row = iota((32, PT), 0).astype(f32).astype(bf16)
    one = jnp.ones((32, PT), bf16)
    zero = jnp.zeros((32, PT), bf16)
    none = jnp.zeros((16, PT), bf16)

    def step(i, carry):
        last, head = carry
        rows = pl.ds(pl.multiple_of(i * 8, 8), 8)
        z = zbin_ref[rows, :]
        weights = corner_weights(frac_ref[0, rows, :], frac_ref[1, rows, :], frac_ref[2, rows, :], mass_ref[rows, :])
        left = []
        right = []
        for e in (0, 1):
            cell = z + e
            upper = (cell >> 5).astype(f32)
            below = jnp.concatenate([upper, upper], axis=0).astype(bf16) == none
            parts = []
            for a in (0, 1):
                for b in (0, 1):
                    terms = jnp.concatenate(two_terms(weights[a][b][e]), axis=0).astype(bf16)
                    parts.append(jnp.where(below, terms, none))
                    parts.append(jnp.where(below, none, terms))
            left.append(jnp.concatenate(parts, axis=0))
            lower = (cell & 31).astype(f32)
            hots = []
            for t in range(8):
                row = jnp.broadcast_to(lower[t:t + 1, :], (32, PT)).astype(bf16)
                hots.append(jnp.where(row == z_row, one, zero))
            right.append(jnp.concatenate(hots, axis=0))
        product = nt_dot(jnp.concatenate(left, axis=1), jnp.concatenate(right, axis=1))
        halves = []
        for a in (0, 1):
            quarters = []
            for q in range(4):
                start = (4 * a + q) * 16
                total = product[start:start + 8, :] + product[start + 8:start + 16, :]
                quarters.append(jnp.where(sub < 4, total[:, 0:128], total[:, 128:256]))
            gathered = None
            for s in range(4):
                value = quarters[s]
                for k in (1, 2, 3):
                    value = jnp.where(four == k, quarters[(k + s) % 4], value)
                if s:
                    value = pltpu.roll(value, 32 * s, 1)
                gathered = value if gathered is None else jnp.where(turn == s, value, gathered)
            halves.append(gathered)
        first = jnp.where(sub < 4, halves[0], pltpu.roll(halves[1], 4, 0))
        second = jnp.where(sub < 4, pltpu.roll(halves[0], 4, 0), halves[1])
        for g, value in ((0, first), (1, second)):
            group = part * (FT // PARTS // 4) + i * 2 + g
            owner = box_ref[group * 4] >> 3
            out_ref[owner, :, pl.ds(pl.multiple_of((group & 3) * 1024, 1024), 1024)] = value.reshape(1, 1024)
            label = jnp.where(four_lanes == (group & 31), label_ref[pl.ds(group >> 5, 1), :], 0.0)
            head = jnp.where(owner == last, head, 0.0) + label
            last = owner
            out_ref[owner, :, 4096:4224] = head
        return last, head

    steps = FT // PARTS // 8
    last, head = lax.fori_loop(0, steps, step, (last_ref[0], head_ref[...]), unroll=steps)
    last_ref[0] = last
    head_ref[...] = head


def fine_profiles(tile_box, fine_column, fine_zbin, fine_frac, fine_weight):
    tiles = FT // PARTS
    return pl.pallas_call(
        fine_profile_kernel,
        out_shape=jax.ShapeDtypeStruct((NODES, 1, LINE), f32),
        grid=(PARTS,),
        in_specs=[
            pl.BlockSpec(memory_space=pltpu.SMEM),
            pl.BlockSpec((FT // 128, 128), lambda i: (0, 0)),
            pl.BlockSpec((FT // 128, 128), lambda i: (0, 0)),
            pl.BlockSpec((tiles, PT), lambda i: (i, 0)),
            pl.BlockSpec((3, tiles, PT), lambda i: (0, i, 0)),
            pl.BlockSpec((tiles, PT), lambda i: (i, 0)),
        ],
        out_specs=pl.BlockSpec((NODES, 1, LINE), lambda i: (0, 0, 0)),
        scratch_shapes=[
            pltpu.VMEM((FT // 128, 128), f32),
            pltpu.VMEM((1, 128), f32),
            pltpu.SMEM((1,), i32),
        ],
        compiler_params=pltpu.CompilerParams(vmem_limit_bytes=VMEM_BYTES),
        cost_estimate=pl.CostEstimate(flops=2 * 128 * 256 * 256 * 112, bytes_accessed=4500000, transcendentals=0),
        name="fine_profiles",
    )(
        tile_box,
        tile_box.reshape(FT // 128, 128),
        fine_column.reshape(FT // 128, 128),
        fine_zbin,
        fine_frac,
        fine_weight,
    )


def tables_kernel(me_ref, home_ref, anchor_ref, owner_ref, place_ref):
    index = iota((8, 128), 0) * 128 + iota((8, 128), 1)
    left = jnp.where(home_ref[...] == me_ref[0], index, NODES * BPH)
    for n in range(BPH):
        box = jnp.minimum(jnp.min(left), NODES * BPH - 1)
        left = jnp.where(left == box, NODES * BPH, left)
        owner_ref[n] = box >> 3
        place_ref[n] = anchor_ref[box]


def tables(me, box_home, box_anchor):
    smem = pl.BlockSpec(memory_space=pltpu.SMEM)
    return pl.pallas_call(
        tables_kernel,
        out_shape=(jax.ShapeDtypeStruct((BPH,), i32), jax.ShapeDtypeStruct((BPH,), i32)),
        in_specs=[smem, pl.BlockSpec(memory_space=pltpu.VMEM), smem],
        out_specs=(smem, smem),
        cost_estimate=pl.CostEstimate(flops=4000000, bytes_accessed=40000, transcendentals=0),
        name="tables",
    )(me, box_home.reshape(8, 128), box_anchor)


def base_kernel(column_ref, zbin_ref, frac_ref, mass_ref, core_ref, front_ref, side_ref, corner_ref, grid_ref):
    grid_ref[...] = jnp.zeros(grid_ref.shape, f32)
    upper_row = iota((8, PT), 0)
    lower_row = iota((128, PT), 0)

    def step(i, carry):
        rows = pl.ds(pl.multiple_of(i * 8, 8), 8)
        z = zbin_ref[rows, :]
        weights = corner_weights(frac_ref[0, rows, :], frac_ref[1, rows, :], frac_ref[2, rows, :], mass_ref[rows, :])
        cells = (z, (z + 1) & (NZ - 1))
        uppers = [cell >> 7 for cell in cells]
        lowers = [cell & 127 for cell in cells]
        for t in range(8):
            left = []
            right = []
            for e in (0, 1):
                mask = jnp.broadcast_to(uppers[e][t:t + 1, :], (8, PT)) == upper_row
                parts = []
                for a in (0, 1):
                    for b in (0, 1):
                        row = jnp.broadcast_to(weights[a][b][e][t:t + 1, :], (8, PT))
                        parts.extend(two_terms(jnp.where(mask, row, 0.0)))
                left.append(jnp.concatenate(parts, axis=0).astype(bf16))
                low = jnp.broadcast_to(lowers[e][t:t + 1, :], (128, PT))
                right.append(jnp.where(low == lower_row, 1.0, 0.0).astype(bf16))
            product = nt_dot(jnp.concatenate(left, axis=1), jnp.concatenate(right, axis=1))
            q = column_ref[i * 8 + t]
            corner = (q // CY) * GY + q % CY
            for a in (0, 1):
                for b in (0, 1):
                    start = (2 * a + b) * 16
                    place = pl.ds(pl.multiple_of((corner + a * GY + b) * 8, 8), 8)
                    grid_ref[place, :] += product[start:start + 8, :] + product[start + 8:start + 16, :]
        return carry

    lax.fori_loop(0, BT // 8, step, 0)
    for x in range(GX):
        for band in range(CY // 8):
            for part in range(8):
                rows = grid_ref[pl.ds((x * GY + band * 8) * 8 + part, 8, stride=8), :]
                if x < CX:
                    core_ref[x, band * 8:band * 8 + 8, part * 128:part * 128 + 128] = rows
                else:
                    front_ref[band * 8:band * 8 + 8, part * 128:part * 128 + 128] = rows
    for part in range(8):
        lanes = slice(part * 128, part * 128 + 128)
        side_ref[:, lanes] = grid_ref[pl.ds(CY * 8 + part, 8, stride=GY * 8), :]
        corner_row = (CX * GY + CY) * 8 + part
        corner_ref[0:1, lanes] = grid_ref[corner_row:corner_row + 1, :]


def base_deposit(base_column, base_zbin, base_frac, base_weight):
    vmem = pl.BlockSpec(memory_space=pltpu.VMEM)
    return pl.pallas_call(
        base_kernel,
        out_shape=(
            jax.ShapeDtypeStruct((CX, CY, NZ), f32),
            jax.ShapeDtypeStruct((CY, NZ), f32),
            jax.ShapeDtypeStruct((CX, NZ), f32),
            jax.ShapeDtypeStruct((1, NZ), f32),
        ),
        in_specs=[pl.BlockSpec(memory_space=pltpu.SMEM), vmem, vmem, vmem],
        out_specs=(vmem, vmem, vmem, vmem),
        scratch_shapes=[pltpu.VMEM((GX * GY * 8, 128), f32)],
        compiler_params=pltpu.CompilerParams(vmem_limit_bytes=VMEM_BYTES),
        cost_estimate=pl.CostEstimate(flops=10000000000, bytes_accessed=5000000, transcendentals=0),
        name="base_deposit",
    )(base_column, base_zbin, base_frac, base_weight)


def halo_kernel(core_ref, front_ref, side_ref, corner_ref, out_ref):
    out_ref[...] = core_ref[...]
    out_ref[0, :, :] += front_ref[...]
    out_ref[:, 0, :] += side_ref[...]
    out_ref[0, 0:1, :] += corner_ref[...]


def halo_add(core, front, side, corner):
    vmem = pl.BlockSpec(memory_space=pltpu.VMEM)
    return pl.pallas_call(
        halo_kernel,
        out_shape=jax.ShapeDtypeStruct((CX, CY, NZ), f32),
        in_specs=[vmem] * 4,
        out_specs=vmem,
        compiler_params=pltpu.CompilerParams(vmem_limit_bytes=VMEM_BYTES),
        cost_estimate=pl.CostEstimate(flops=1000000, bytes_accessed=4500000, transcendentals=0),
        name="halo_add",
    )(core, front, side, corner)


ROWS = NODES * SLOTS * 8
MB = 256
KB = 512


def arrival_rows(heads):
    line = iota((128, 128), 0)
    lane = iota((128, 128), 1)
    spread = jnp.where(line % 16 == (lane // 8) % 4 * 4 + lane % 4, 1.0, 0.0).astype(bf16)
    labels = (heads + 0.5).astype(i32)
    digits = jnp.concatenate([(labels >> 4).astype(f32), (labels & 15).astype(f32)], axis=0).astype(bf16)
    wide = jnp.dot(digits, spread, preferred_element_type=f32)
    wide = wide[0:16, :] * 16.0 + wide[16:32, :]
    wide = jnp.where(iota((16, 128), 0) % 4 == iota((16, 128), 1) // 32, wide, 0.0)
    shift = 64 * ((iota((1, 128), 1) // 4) % 2)
    return [
        (jnp.sum(wide[4 * k:4 * k + 4, :], axis=0, keepdims=True) + 0.5).astype(i32) + shift for k in range(4)
    ]


def arrival_terms(got_ref):
    count = got_ref.shape[0]
    parts = [got_ref[s, :, 0:SLOTS * 1024].reshape(SLOTS * 8, 128) for s in range(count)]
    high, low = two_terms(jnp.concatenate(parts, axis=0))
    return high.astype(bf16), low.astype(bf16)


def coarse_kernel(home_ref, got_ref, send_ref, head_ref, sums_ref, part_ref, sem):
    step = pl.program_id(0)
    terms = jnp.concatenate(arrival_terms(got_ref), axis=1)
    lines = []
    for k, row in enumerate(arrival_rows(got_ref[:, 0, SLOTS * 1024:LINE])):
        head_ref[pl.ds(step * (KB // 128) + k, 1), :] = row
        lines.append((row >> 10) * 512 + ((row >> 7) & 7) * 64 + (row & 63))

    @pl.when(step == 0)
    def _():
        sums_ref[...] = jnp.zeros(sums_ref.shape, f32)

    for m in range(1024 // MB):
        target = iota((MB, 128), 0) + m * MB
        hot = jnp.concatenate(
            [jnp.where(jnp.broadcast_to(line, (MB, 128)) == target, 1.0, 0.0).astype(bf16) for line in lines], axis=1
        )
        product = jnp.dot(hot, terms, preferred_element_type=f32)
        sums_ref[m * MB:(m + 1) * MB, :] += product[:, 0:128] + product[:, 128:256]

    @pl.when(step == ROWS // KB - 1)
    def _():
        lane = iota((64, 128), 1)
        fold_row = iota((512, 128), 0)
        fold_lane = iota((512, 128), 1)
        fold = jnp.where((fold_row // 128) * 32 + (fold_row % 64) // 2 == fold_lane, 1.0, 0.0).astype(bf16)
        for far in (0, 1):
            pieces = []
            for q in range(4):
                spot = (4 * far + q) * 64
                odd = sums_ref[512 + spot:512 + spot + 64, :]
                before = jnp.concatenate([jnp.zeros((8, 128), f32), odd[0:56, :]], axis=0)
                both = sums_ref[spot:spot + 64, :] + jnp.where(lane < 64, odd, before)
                pieces.append(jnp.concatenate(two_terms(both), axis=0).astype(bf16))
            folded = jnp.dot(jnp.concatenate(pieces, axis=1), fold, preferred_element_type=f32)
            part_ref[far * 64:far * 64 + 64, :] = folded[0:64, :] + folded[64:128, :]
        copies = []
        for box in range(BPH):
            for far in (0, 1):
                hot = part_ref[pl.ds(far * 64 + box, 8, stride=8), :]
                part_ref[128 + box * 16 + far * 8:128 + box * 16 + far * 8 + 8, :] = hot
        for box in range(BPH):
            copy = pltpu.make_async_copy(
                part_ref.at[pl.ds(128 + box * 16, 16), :], send_ref.at[home_ref[box]], sem.at[box]
            )
            copy.start()
            copies.append(copy)
        for copy in copies:
            copy.wait()


def coarse_deposit(homes, arrived):
    return pl.pallas_call(
        coarse_kernel,
        out_shape=(jax.ShapeDtypeStruct((NODES, 16, 128), f32), jax.ShapeDtypeStruct((32, 128), i32)),
        grid=(ROWS // KB,),
        in_specs=[
            pl.BlockSpec(memory_space=pltpu.SMEM),
            pl.BlockSpec((16, 1, LINE), lambda i: (i, 0, 0)),
        ],
        out_specs=(pl.BlockSpec(memory_space=pl.ANY), pl.BlockSpec((32, 128), lambda i: (0, 0))),
        scratch_shapes=[
            pltpu.VMEM((1024, 128), f32),
            pltpu.VMEM((256, 128), f32),
            pltpu.SemaphoreType.DMA((BPH,)),
        ],
        compiler_params=pltpu.CompilerParams(vmem_limit_bytes=VMEM_BYTES),
        cost_estimate=pl.CostEstimate(flops=2 * 1024 * ROWS * 256, bytes_accessed=2200000, transcendentals=0),
        name="coarse_deposit",
    )(homes, arrived)


def fine_kernel(head_ref, got_ref, fine_ref, terms_ref, sums_ref, hot_ref):
    high, low = arrival_terms(got_ref)
    terms_ref[:, 0:128] = high
    terms_ref[:, 128:256] = low

    def block(m, carry):
        target = iota((MB, 128), 0) + m * MB
        for k in range(ROWS // 128):
            row = jnp.broadcast_to(head_ref[k:k + 1, :], (MB, 128))
            hot_ref[:, k * 128:k * 128 + 128] = jnp.where(row == target, 1.0, 0.0).astype(bf16)
        product = jnp.dot(hot_ref[...], terms_ref[...], preferred_element_type=f32)
        sums_ref[pl.ds(pl.multiple_of(m * MB, MB), MB), :] = product[:, 0:128] + product[:, 128:256]
        return carry

    lax.fori_loop(0, 2048 // MB, block, 0)
    lane = iota((8, 128), 1)
    for x in range(16):
        for y in range(8):
            spot = (x * 8 + y) * 8
            odd = sums_ref[1024 + spot:1024 + spot + 8, :]
            before = sums_ref[1024 + spot - 8:1024 + spot, :] if y else jnp.zeros((8, 128), f32)
            cross = pltpu.roll(jnp.where(lane < 64, odd, before), 64, 1)
            fine_ref[:, spot * 16:spot * 16 + 128] = sums_ref[spot:spot + 8, :] + cross


def fine_deposit(header, arrived):
    vmem = pl.BlockSpec(memory_space=pltpu.VMEM)
    return pl.pallas_call(
        fine_kernel,
        out_shape=jax.ShapeDtypeStruct((BPH, 16384), f32),
        in_specs=[vmem, vmem],
        out_specs=vmem,
        scratch_shapes=[
            pltpu.VMEM((ROWS, 256), bf16),
            pltpu.VMEM((2048, 128), f32),
            pltpu.VMEM((MB, ROWS), bf16),
        ],
        compiler_params=pltpu.CompilerParams(vmem_limit_bytes=VMEM_BYTES),
        cost_estimate=pl.CostEstimate(flops=2 * 2048 * ROWS * 256, bytes_accessed=4000000, transcendentals=0),
        name="fine_deposit",
    )(header, arrived)


def lattice_kernel(owner_ref, place_ref, base_ref, got_ref, out_ref, held_ref, block_ref, got_sem, in_sem, out_sem):
    def spot_of(n, grid):
        place = place_ref[n]
        rows = pl.ds(pl.multiple_of(((place >> 5) & 7) * 8, 8), 8)
        lanes = pl.ds(pl.multiple_of(((place >> 2) & 7) * 128, 128), 128)
        return grid.at[:, rows, lanes]

    copies = []
    for n in range(BPH):
        copies.append(pltpu.make_async_copy(got_ref.at[owner_ref[n]], held_ref.at[n], got_sem.at[n]))
        copies.append(pltpu.make_async_copy(spot_of(n, base_ref), block_ref.at[n], in_sem.at[n]))
    for copy in copies:
        copy.start()
    firsts = []
    for n in range(BPH):
        first = jnp.int32(n)
        for k in reversed(range(n)):
            first = jnp.where(place_ref[k] >> 2 == place_ref[n] >> 2, k, first)
        firsts.append(first)
    for copy in copies:
        copy.wait()
    quarter = iota((8, 128), 1) // 32
    for n in range(BPH):
        spot = place_ref[n] & 3
        for x in range(CX):
            value = held_ref[n, (x // 4) * 8:(x // 4) * 8 + 8, :]
            moved = pltpu.roll(value, ((spot - x % 4 + 4) & 3) * 32, 1)
            block_ref[firsts[n], x] += jnp.where(quarter == spot, moved, 0.0)
    for n in range(BPH):
        @pl.when(firsts[n] == n)
        def _():
            pltpu.make_async_copy(block_ref.at[n], spot_of(n, out_ref), out_sem.at[n]).start()
    for n in range(BPH):
        @pl.when(firsts[n] == n)
        def _():
            pltpu.make_async_copy(block_ref.at[n], spot_of(n, out_ref), out_sem.at[n]).wait()


def lattice_add(owners, places, base, arrived):
    smem = pl.BlockSpec(memory_space=pltpu.SMEM)
    hbm = pl.BlockSpec(memory_space=pl.ANY)
    return pl.pallas_call(
        lattice_kernel,
        out_shape=jax.ShapeDtypeStruct((CX, CY, NZ), f32),
        in_specs=[smem, smem, hbm, hbm],
        out_specs=hbm,
        input_output_aliases={2: 0},
        scratch_shapes=[
            pltpu.VMEM((BPH, 16, 128), f32),
            pltpu.VMEM((BPH, CX, 8, 128), f32),
            pltpu.SemaphoreType.DMA((BPH,)),
            pltpu.SemaphoreType.DMA((BPH,)),
            pltpu.SemaphoreType.DMA((BPH,)),
        ],
        compiler_params=pltpu.CompilerParams(vmem_limit_bytes=VMEM_BYTES),
        cost_estimate=pl.CostEstimate(flops=1000000, bytes_accessed=1000000, transcendentals=0),
        name="lattice_add",
    )(owners, places, base, arrived)


def shards(
    base_column,
    base_zbin,
    base_frac,
    base_weight,
    fine_column,
    fine_zbin,
    fine_frac,
    fine_weight,
    tile_box,
    box_home,
    box_anchor,
):
    myself = lax.axis_index(AXES).astype(i32)
    homes = lax.dynamic_slice_in_dim(box_home, myself * BPH, BPH, 0)
    outgoing = fine_profiles(tile_box, fine_column, fine_zbin, fine_frac, fine_weight)
    outgoing, base_column, myself = lax.optimization_barrier((outgoing, base_column, myself))
    arrived = lax.all_to_all(outgoing, AXES, split_axis=0, concat_axis=0, tiled=True)
    owners, places = tables(myself.reshape(1), box_home, box_anchor)
    core, front, side, corner = base_deposit(base_column, base_zbin, base_frac, base_weight)
    front = shifted(front, "blk", 1)
    side = shifted(side, "cross", 1)
    corner = diagonal(corner)
    arrived, core, front, side, corner, owners, places = lax.optimization_barrier(
        (arrived, core, front, side, corner, owners, places)
    )
    sending, header = coarse_deposit(homes, arrived)
    sending, header, core = lax.optimization_barrier((sending, header, core))
    returned = lax.all_to_all(sending, AXES, split_axis=0, concat_axis=0, tiled=True)
    fine_rows = fine_deposit(header, arrived)
    base = halo_add(core, front, side, corner)
    returned, base, fine_rows = lax.optimization_barrier((returned, base, fine_rows))
    base_out = lattice_add(owners, places, base, returned)
    return (base_out, fine_rows)


def solution(mesh):
    placed = (
        P(("blk", "cross")),
        P(("blk", "cross"), None),
        P(None, ("blk", "cross"), None),
        P(("blk", "cross"), None),
        P(("blk", "cross")),
        P(("blk", "cross"), None),
        P(None, ("blk", "cross"), None),
        P(("blk", "cross"), None),
        P(("blk", "cross")),
        P(),
        P(),
    )
    return jax.shard_map(
        shards,
        mesh=mesh,
        in_specs=placed,
        out_specs=(P("blk", "cross", None), P(("blk", "cross"), None)),
        check_vma=False,
    )
```

```python
import jax
import jax.numpy as jnp
from jax import lax
from jax.experimental import pallas as pl
from jax.experimental.pallas import tpu as pltpu
from jax.sharding import PartitionSpec as P

CX = 8
CY = 64
NZ = 1024
BPH = 8
NODES = 128
PT = 128
BT = 256
FT = 896
GROUPS = FT // 4
SLOTS = 4
GX = CX + 1
GY = CY + 1
AXES = ("blk", "cross")
PARTS = 4
LINE = SLOTS * 1024 + 128
VMEM_BYTES = 62 * 1024 * 1024
HALF_VMEM = 32 * 1024 * 1024
f32 = jnp.float32
bf16 = jnp.bfloat16
i32 = jnp.int32


def shifted(value, axis, steps):
    count = lax.axis_size(axis)
    pairs = [(source, (source + steps) % count) for source in range(count)]
    return lax.ppermute(value, axis, pairs)


def diagonal(value):
    blocks, columns = lax.axis_size("blk"), lax.axis_size("cross")
    pairs = [
        (b * columns + c, (b + 1) % blocks * columns + (c + 1) % columns)
        for b in range(blocks)
        for c in range(columns)
    ]
    return lax.ppermute(value, AXES, pairs)


def iota(shape, dim):
    return lax.broadcasted_iota(i32, shape, dim)


def two_terms(value):
    high = value.astype(bf16).astype(f32)
    return high, value - high


def nt_dot(left, right):
    return lax.dot_general(left, right, (((1,), (1,)), ((), ())), preferred_element_type=f32)


def corner_weights(u, v, w, m):
    result = []
    for part_x in (1.0 - u, u):
        row = []
        for part_y in (1.0 - v, v):
            plane = m * part_x * part_y
            row.append((plane * (1.0 - w), plane * w))
        result.append(row)
    return result


def fine_profile_kernel(
    box_ref, boxes_ref, columns_ref, zbin_ref, frac_ref, mass_ref, out_ref, label_ref, head_ref, last_ref
):
    part = pl.program_id(0)

    @pl.when(part == 0)
    def _():
        out_ref[...] = jnp.zeros(out_ref.shape, f32)
        boxes = boxes_ref[...]
        columns = columns_ref[...]
        x = (columns * 4370) >> 16
        y = columns - x * 15
        label_ref[...] = ((y & 1) * 1024 + (x * 8 + (y >> 1)) * 8 + (boxes & 7)).astype(f32)
        head_ref[...] = jnp.zeros((1, 128), f32)
        last_ref[0] = -1

    four_lanes = iota((1, 128), 1) // 4
    sub = iota((8, PT), 0)
    four = sub % 4
    turn = (iota((8, PT), 1) // 32 - four) & 3
    z_row = iota((32, PT), 0).astype(f32).astype(bf16)
    one = jnp.ones((32, PT), bf16)
    zero = jnp.zeros((32, PT), bf16)
    none = jnp.zeros((16, PT), bf16)

    def step(i, carry):
        last, head = carry
        rows = pl.ds(pl.multiple_of(i * 8, 8), 8)
        z = zbin_ref[rows, :]
        weights = corner_weights(frac_ref[0, rows, :], frac_ref[1, rows, :], frac_ref[2, rows, :], mass_ref[rows, :])
        left = []
        right = []
        for e in (0, 1):
            cell = z + e
            upper = (cell >> 5).astype(f32)
            below = jnp.concatenate([upper, upper], axis=0).astype(bf16) == none
            parts = []
            for a in (0, 1):
                for b in (0, 1):
                    terms = jnp.concatenate(two_terms(weights[a][b][e]), axis=0).astype(bf16)
                    parts.append(jnp.where(below, terms, none))
                    parts.append(jnp.where(below, none, terms))
            left.append(jnp.concatenate(parts, axis=0))
            lower = (cell & 31).astype(f32)
            hots = []
            for t in range(8):
                row = jnp.broadcast_to(lower[t:t + 1, :], (32, PT)).astype(bf16)
                hots.append(jnp.where(row == z_row, one, zero))
            right.append(jnp.concatenate(hots, axis=0))
        product = nt_dot(jnp.concatenate(left, axis=1), jnp.concatenate(right, axis=1))
        halves = []
        for a in (0, 1):
            quarters = []
            for q in range(4):
                start = (4 * a + q) * 16
                total = product[start:start + 8, :] + product[start + 8:start + 16, :]
                quarters.append(jnp.where(sub < 4, total[:, 0:128], total[:, 128:256]))
            gathered = None
            for s in range(4):
                value = quarters[s]
                for k in (1, 2, 3):
                    value = jnp.where(four == k, quarters[(k + s) % 4], value)
                if s:
                    value = pltpu.roll(value, 32 * s, 1)
                gathered = value if gathered is None else jnp.where(turn == s, value, gathered)
            halves.append(gathered)
        first = jnp.where(sub < 4, halves[0], pltpu.roll(halves[1], 4, 0))
        second = jnp.where(sub < 4, pltpu.roll(halves[0], 4, 0), halves[1])
        for g, value in ((0, first), (1, second)):
            group = part * (FT // PARTS // 4) + i * 2 + g
            owner = box_ref[group * 4] >> 3
            out_ref[owner, :, pl.ds(pl.multiple_of((group & 3) * 1024, 1024), 1024)] = value.reshape(1, 1024)
            label = jnp.where(four_lanes == (group & 31), label_ref[pl.ds(group >> 5, 1), :], 0.0)
            head = jnp.where(owner == last, head, 0.0) + label
            last = owner
            out_ref[owner, :, 4096:4224] = head
        return last, head

    steps = FT // PARTS // 8
    last, head = lax.fori_loop(0, steps, step, (last_ref[0], head_ref[...]), unroll=steps)
    last_ref[0] = last
    head_ref[...] = head


def fine_profiles(tile_box, fine_column, fine_zbin, fine_frac, fine_weight):
    tiles = FT // PARTS
    return pl.pallas_call(
        fine_profile_kernel,
        out_shape=jax.ShapeDtypeStruct((NODES, 1, LINE), f32),
        grid=(PARTS,),
        in_specs=[
            pl.BlockSpec(memory_space=pltpu.SMEM),
            pl.BlockSpec((FT // 128, 128), lambda i: (0, 0)),
            pl.BlockSpec((FT // 128, 128), lambda i: (0, 0)),
            pl.BlockSpec((tiles, PT), lambda i: (i, 0)),
            pl.BlockSpec((3, tiles, PT), lambda i: (0, i, 0)),
            pl.BlockSpec((tiles, PT), lambda i: (i, 0)),
        ],
        out_specs=pl.BlockSpec((NODES, 1, LINE), lambda i: (0, 0, 0)),
        scratch_shapes=[
            pltpu.VMEM((FT // 128, 128), f32),
            pltpu.VMEM((1, 128), f32),
            pltpu.SMEM((1,), i32),
        ],
        compiler_params=pltpu.CompilerParams(vmem_limit_bytes=VMEM_BYTES),
        cost_estimate=pl.CostEstimate(flops=2 * 128 * 256 * 256 * 112, bytes_accessed=4500000, transcendentals=0),
        name="fine_profiles",
    )(
        tile_box,
        tile_box.reshape(FT // 128, 128),
        fine_column.reshape(FT // 128, 128),
        fine_zbin,
        fine_frac,
        fine_weight,
    )


def tables_kernel(me_ref, home_ref, anchor_ref, owner_ref, place_ref):
    index = iota((8, 128), 0) * 128 + iota((8, 128), 1)
    left = jnp.where(home_ref[...] == me_ref[0], index, NODES * BPH)
    for n in range(BPH):
        box = jnp.minimum(jnp.min(left), NODES * BPH - 1)
        left = jnp.where(left == box, NODES * BPH, left)
        owner_ref[n] = box >> 3
        place_ref[n] = anchor_ref[box]


def tables(me, box_home, box_anchor):
    smem = pl.BlockSpec(memory_space=pltpu.SMEM)
    return pl.pallas_call(
        tables_kernel,
        out_shape=(jax.ShapeDtypeStruct((BPH,), i32), jax.ShapeDtypeStruct((BPH,), i32)),
        in_specs=[smem, pl.BlockSpec(memory_space=pltpu.VMEM), smem],
        out_specs=(smem, smem),
        cost_estimate=pl.CostEstimate(flops=4000000, bytes_accessed=40000, transcendentals=0),
        name="tables",
    )(me, box_home.reshape(8, 128), box_anchor)


def base_kernel(column_ref, zbin_ref, frac_ref, mass_ref, core_ref, front_ref, side_ref, corner_ref, grid_ref):
    grid_ref[...] = jnp.zeros(grid_ref.shape, f32)
    upper_row = iota((8, PT), 0)
    lower_row = iota((128, PT), 0)

    def step(i, carry):
        rows = pl.ds(pl.multiple_of(i * 8, 8), 8)
        z = zbin_ref[rows, :]
        weights = corner_weights(frac_ref[0, rows, :], frac_ref[1, rows, :], frac_ref[2, rows, :], mass_ref[rows, :])
        cells = (z, (z + 1) & (NZ - 1))
        uppers = [cell >> 7 for cell in cells]
        lowers = [cell & 127 for cell in cells]
        for t in range(8):
            left = []
            right = []
            for e in (0, 1):
                mask = jnp.broadcast_to(uppers[e][t:t + 1, :], (8, PT)) == upper_row
                parts = []
                for a in (0, 1):
                    for b in (0, 1):
                        row = jnp.broadcast_to(weights[a][b][e][t:t + 1, :], (8, PT))
                        parts.extend(two_terms(jnp.where(mask, row, 0.0)))
                left.append(jnp.concatenate(parts, axis=0).astype(bf16))
                low = jnp.broadcast_to(lowers[e][t:t + 1, :], (128, PT))
                right.append(jnp.where(low == lower_row, 1.0, 0.0).astype(bf16))
            product = nt_dot(jnp.concatenate(left, axis=1), jnp.concatenate(right, axis=1))
            q = column_ref[i * 8 + t]
            corner = (q // CY) * GY + q % CY
            for a in (0, 1):
                for b in (0, 1):
                    start = (2 * a + b) * 16
                    place = pl.ds(pl.multiple_of((corner + a * GY + b) * 8, 8), 8)
                    grid_ref[place, :] += product[start:start + 8, :] + product[start + 8:start + 16, :]
        return carry

    lax.fori_loop(0, BT // 8, step, 0)
    for x in range(GX):
        for band in range(CY // 8):
            for part in range(8):
                rows = grid_ref[pl.ds((x * GY + band * 8) * 8 + part, 8, stride=8), :]
                if x < CX:
                    core_ref[x, band * 8:band * 8 + 8, part * 128:part * 128 + 128] = rows
                else:
                    front_ref[band * 8:band * 8 + 8, part * 128:part * 128 + 128] = rows
    for part in range(8):
        lanes = slice(part * 128, part * 128 + 128)
        side_ref[:, lanes] = grid_ref[pl.ds(CY * 8 + part, 8, stride=GY * 8), :]
        corner_row = (CX * GY + CY) * 8 + part
        corner_ref[0:1, lanes] = grid_ref[corner_row:corner_row + 1, :]


def base_deposit(base_column, base_zbin, base_frac, base_weight):
    vmem = pl.BlockSpec(memory_space=pltpu.VMEM)
    return pl.pallas_call(
        base_kernel,
        out_shape=(
            jax.ShapeDtypeStruct((CX, CY, NZ), f32),
            jax.ShapeDtypeStruct((CY, NZ), f32),
            jax.ShapeDtypeStruct((CX, NZ), f32),
            jax.ShapeDtypeStruct((1, NZ), f32),
        ),
        in_specs=[pl.BlockSpec(memory_space=pltpu.SMEM), vmem, vmem, vmem],
        out_specs=(vmem, vmem, vmem, vmem),
        scratch_shapes=[pltpu.VMEM((GX * GY * 8, 128), f32)],
        compiler_params=pltpu.CompilerParams(vmem_limit_bytes=HALF_VMEM),
        cost_estimate=pl.CostEstimate(flops=10000000000, bytes_accessed=5000000, transcendentals=0),
        name="base_deposit",
    )(base_column, base_zbin, base_frac, base_weight)


def halo_kernel(core_ref, front_ref, side_ref, corner_ref, out_ref, face_ref, band_ref, sem):
    slab = pltpu.make_async_copy(core_ref.at[0], face_ref, sem.at[0])
    band = pltpu.make_async_copy(core_ref.at[pl.ds(1, CX - 1), pl.ds(0, 8), :], band_ref, sem.at[1])
    slab.start()
    band.start()
    slab.wait()
    face_ref[...] += front_ref[...]
    face_ref[0:1, :] += side_ref[0:1, :] + corner_ref[...]
    slab_out = pltpu.make_async_copy(face_ref, out_ref.at[0], sem.at[2])
    slab_out.start()
    band.wait()
    for x in range(1, CX):
        band_ref[x - 1, 0:1, :] += side_ref[x:x + 1, :]
    band_out = pltpu.make_async_copy(band_ref, out_ref.at[pl.ds(1, CX - 1), pl.ds(0, 8), :], sem.at[3])
    band_out.start()
    slab_out.wait()
    band_out.wait()


def halo_add(core, front, side, corner):
    vmem = pl.BlockSpec(memory_space=pltpu.VMEM)
    hbm = pl.BlockSpec(memory_space=pltpu.HBM)
    return pl.pallas_call(
        halo_kernel,
        out_shape=jax.ShapeDtypeStruct((CX, CY, NZ), f32),
        in_specs=[hbm, vmem, vmem, vmem],
        out_specs=hbm,
        input_output_aliases={0: 0},
        scratch_shapes=[
            pltpu.VMEM((CY, NZ), f32),
            pltpu.VMEM((CX - 1, 8, NZ), f32),
            pltpu.SemaphoreType.DMA((4,)),
        ],
        compiler_params=pltpu.CompilerParams(vmem_limit_bytes=HALF_VMEM),
        cost_estimate=pl.CostEstimate(flops=1000000, bytes_accessed=1500000, transcendentals=0),
        name="halo_add",
    )(core, front, side, corner)


ROWS = NODES * SLOTS * 8
MB = 256


def arrival_rows(heads):
    count = heads.shape[0]
    line = iota((128, 128), 0)
    lane = iota((128, 128), 1)
    spread = jnp.where(line % 16 == (lane // 8) % 4 * 4 + lane % 4, 1.0, 0.0).astype(bf16)
    labels = (heads + 0.5).astype(i32)
    digits = jnp.concatenate([(labels >> 4).astype(f32), (labels & 15).astype(f32)], axis=0).astype(bf16)
    wide = jnp.dot(digits, spread, preferred_element_type=f32)
    wide = wide[0:count, :] * 16.0 + wide[count:2 * count, :]
    wide = jnp.where(iota((count, 128), 0) % 4 == iota((count, 128), 1) // 32, wide, 0.0)
    shift = 64 * ((iota((1, 128), 1) // 4) % 2)
    return [
        (jnp.sum(wide[4 * k:4 * k + 4, :], axis=0, keepdims=True) + 0.5).astype(i32) + shift
        for k in range(count // 4)
    ]


def one_hot(lines, target):
    one = jnp.ones(target.shape, bf16)
    zero = jnp.zeros(target.shape, bf16)
    return jnp.concatenate(
        [jnp.where(jnp.broadcast_to(line, target.shape).astype(jnp.int16) == target, one, zero) for line in lines],
        axis=1,
    )


def arrival_terms(got_ref, first, count):
    parts = [got_ref[s, :, 0:SLOTS * 1024].reshape(SLOTS * 8, 128) for s in range(first, first + count)]
    high, low = two_terms(jnp.concatenate(parts, axis=0))
    return jnp.concatenate([high.astype(bf16), low.astype(bf16)], axis=1)


def coarse_kernel(home_ref, got_ref, send_ref, head_ref, sums_ref, part_ref, sem):
    terms = arrival_terms(got_ref, 0, NODES)
    lines = []
    for k, row in enumerate(arrival_rows(got_ref[:, 0, SLOTS * 1024:LINE])):
        head_ref[k:k + 1, :] = row
        lines.append((row >> 10) * 512 + ((row >> 7) & 7) * 64 + (row & 63))
    for m in range(1024 // MB):
        target = (iota((MB, 128), 0) + m * MB).astype(jnp.int16)
        product = jnp.dot(one_hot(lines, target), terms, preferred_element_type=f32)
        sums_ref[m * MB:(m + 1) * MB, :] = product[:, 0:128] + product[:, 128:256]
    lane = iota((64, 128), 1)
    fold_row = iota((512, 128), 0)
    fold_lane = iota((512, 128), 1)
    fold = jnp.where((fold_row // 128) * 32 + (fold_row % 64) // 2 == fold_lane, 1.0, 0.0).astype(bf16)
    for far in (0, 1):
        pieces = []
        for q in range(4):
            spot = (4 * far + q) * 64
            odd = sums_ref[512 + spot:512 + spot + 64, :]
            before = jnp.concatenate([jnp.zeros((8, 128), f32), odd[0:56, :]], axis=0)
            both = sums_ref[spot:spot + 64, :] + jnp.where(lane < 64, odd, before)
            pieces.append(jnp.concatenate(two_terms(both), axis=0).astype(bf16))
        folded = jnp.dot(jnp.concatenate(pieces, axis=1), fold, preferred_element_type=f32)
        part_ref[far * 64:far * 64 + 64, :] = folded[0:64, :] + folded[64:128, :]
    copies = []
    for box in range(BPH):
        for far in (0, 1):
            hot = part_ref[pl.ds(far * 64 + box, 8, stride=8), :]
            part_ref[128 + box * 16 + far * 8:128 + box * 16 + far * 8 + 8, :] = hot
    for box in range(BPH):
        copy = pltpu.make_async_copy(
            part_ref.at[pl.ds(128 + box * 16, 16), :], send_ref.at[home_ref[box]], sem.at[box]
        )
        copy.start()
        copies.append(copy)
    for copy in copies:
        copy.wait()


def coarse_deposit(homes, arrived):
    hbm = pl.BlockSpec(memory_space=pltpu.HBM)
    return pl.pallas_call(
        coarse_kernel,
        out_shape=(jax.ShapeDtypeStruct((NODES, 16, 128), f32), jax.ShapeDtypeStruct((32, 128), i32)),
        in_specs=[pl.BlockSpec(memory_space=pltpu.SMEM), pl.BlockSpec(memory_space=pltpu.VMEM)],
        out_specs=(hbm, pl.BlockSpec(memory_space=pltpu.VMEM)),
        scratch_shapes=[
            pltpu.VMEM((1024, 128), f32),
            pltpu.VMEM((256, 128), f32),
            pltpu.SemaphoreType.DMA((BPH,)),
        ],
        compiler_params=pltpu.CompilerParams(vmem_limit_bytes=HALF_VMEM),
        cost_estimate=pl.CostEstimate(flops=2 * 1024 * ROWS * 256, bytes_accessed=2200000, transcendentals=0),
        name="coarse_deposit",
    )(homes, arrived)


def fine_kernel(head_ref, got_ref, fine_ref, terms_ref, sums_ref, hot_ref):
    terms_ref[...] = arrival_terms(got_ref, 0, NODES)

    def block(m, carry):
        target = (iota((MB, 128), 0) + m * MB).astype(jnp.int16)
        hot_ref[...] = one_hot([head_ref[k:k + 1, :] for k in range(ROWS // 128)], target)
        product = jnp.dot(hot_ref[...], terms_ref[...], preferred_element_type=f32)
        sums_ref[pl.ds(pl.multiple_of(m * MB, MB), MB), :] = product[:, 0:128] + product[:, 128:256]
        return carry

    lax.fori_loop(0, 2048 // MB, block, 0)
    lane = iota((8, 128), 1)
    for x in range(16):
        for y in range(8):
            spot = (x * 8 + y) * 8
            odd = sums_ref[1024 + spot:1024 + spot + 8, :]
            before = sums_ref[1024 + spot - 8:1024 + spot, :] if y else jnp.zeros((8, 128), f32)
            cross = pltpu.roll(jnp.where(lane < 64, odd, before), 64, 1)
            fine_ref[:, spot * 16:spot * 16 + 128] = sums_ref[spot:spot + 8, :] + cross


def fine_deposit(header, arrived):
    vmem = pl.BlockSpec(memory_space=pltpu.VMEM)
    return pl.pallas_call(
        fine_kernel,
        out_shape=jax.ShapeDtypeStruct((BPH, 16384), f32),
        in_specs=[vmem, vmem],
        out_specs=vmem,
        scratch_shapes=[
            pltpu.VMEM((ROWS, 256), bf16),
            pltpu.VMEM((2048, 128), f32),
            pltpu.VMEM((MB, ROWS), bf16),
        ],
        compiler_params=pltpu.CompilerParams(vmem_limit_bytes=HALF_VMEM),
        cost_estimate=pl.CostEstimate(flops=2 * 2048 * ROWS * 256, bytes_accessed=4000000, transcendentals=0),
        name="fine_deposit",
    )(header, arrived)


def lattice_kernel(owner_ref, place_ref, base_ref, got_ref, out_ref, held_ref, block_ref, got_sem, in_sem, out_sem):
    def spot_of(n, grid):
        place = place_ref[n]
        rows = pl.ds(pl.multiple_of(((place >> 5) & 7) * 8, 8), 8)
        lanes = pl.ds(pl.multiple_of(((place >> 2) & 7) * 128, 128), 128)
        return grid.at[:, rows, lanes]

    copies = []
    for n in range(BPH):
        copies.append(pltpu.make_async_copy(got_ref.at[owner_ref[n]], held_ref.at[n], got_sem.at[n]))
        copies.append(pltpu.make_async_copy(spot_of(n, base_ref), block_ref.at[n], in_sem.at[n]))
    for copy in copies:
        copy.start()
    firsts = []
    for n in range(BPH):
        first = jnp.int32(n)
        for k in reversed(range(n)):
            first = jnp.where(place_ref[k] >> 2 == place_ref[n] >> 2, k, first)
        firsts.append(first)
    for copy in copies:
        copy.wait()
    quarter = iota((8, 128), 1) // 32
    for n in range(BPH):
        spot = place_ref[n] & 3
        for x in range(CX):
            value = held_ref[n, (x // 4) * 8:(x // 4) * 8 + 8, :]
            moved = pltpu.roll(value, ((spot - x % 4 + 4) & 3) * 32, 1)
            block_ref[firsts[n], x] += jnp.where(quarter == spot, moved, 0.0)
    for n in range(BPH):
        @pl.when(firsts[n] == n)
        def _():
            pltpu.make_async_copy(block_ref.at[n], spot_of(n, out_ref), out_sem.at[n]).start()
    for n in range(BPH):
        @pl.when(firsts[n] == n)
        def _():
            pltpu.make_async_copy(block_ref.at[n], spot_of(n, out_ref), out_sem.at[n]).wait()


def lattice_add(owners, places, base, arrived):
    smem = pl.BlockSpec(memory_space=pltpu.SMEM)
    hbm = pl.BlockSpec(memory_space=pltpu.HBM)
    return pl.pallas_call(
        lattice_kernel,
        out_shape=jax.ShapeDtypeStruct((CX, CY, NZ), f32),
        in_specs=[smem, smem, hbm, hbm],
        out_specs=hbm,
        input_output_aliases={2: 0},
        scratch_shapes=[
            pltpu.VMEM((BPH, 16, 128), f32),
            pltpu.VMEM((BPH, CX, 8, 128), f32),
            pltpu.SemaphoreType.DMA((BPH,)),
            pltpu.SemaphoreType.DMA((BPH,)),
            pltpu.SemaphoreType.DMA((BPH,)),
        ],
        compiler_params=pltpu.CompilerParams(vmem_limit_bytes=VMEM_BYTES),
        cost_estimate=pl.CostEstimate(flops=1000000, bytes_accessed=1000000, transcendentals=0),
        name="lattice_add",
    )(owners, places, base, arrived)


def shards(
    base_column,
    base_zbin,
    base_frac,
    base_weight,
    fine_column,
    fine_zbin,
    fine_frac,
    fine_weight,
    tile_box,
    box_home,
    box_anchor,
):
    myself = lax.axis_index(AXES).astype(i32)
    homes = lax.dynamic_slice_in_dim(box_home, myself * BPH, BPH, 0)
    outgoing = fine_profiles(tile_box, fine_column, fine_zbin, fine_frac, fine_weight)
    outgoing, base_column, myself = lax.optimization_barrier((outgoing, base_column, myself))
    arrived = lax.all_to_all(outgoing, AXES, split_axis=0, concat_axis=0, tiled=True)
    owners, places = tables(myself.reshape(1), box_home, box_anchor)
    core, front, side, corner = base_deposit(base_column, base_zbin, base_frac, base_weight)
    arrived, core, front, side, corner, owners, places = lax.optimization_barrier(
        (arrived, core, front, side, corner, owners, places)
    )
    sending, header = coarse_deposit(homes, arrived)
    sending, header, front, side, corner = lax.optimization_barrier((sending, header, front, side, corner))
    returned = lax.all_to_all(sending, AXES, split_axis=0, concat_axis=0, tiled=True)
    front = shifted(front, "blk", 1)
    side = shifted(side, "cross", 1)
    corner = diagonal(corner)
    fine_rows = fine_deposit(header, arrived)
    front, side, corner, fine_rows = lax.optimization_barrier((front, side, corner, fine_rows))
    base = halo_add(core, front, side, corner)
    returned, base, fine_rows = lax.optimization_barrier((returned, base, fine_rows))
    base_out = lattice_add(owners, places, base, returned)
    return (base_out, fine_rows)


def solution(mesh):
    placed = (
        P(("blk", "cross")),
        P(("blk", "cross"), None),
        P(None, ("blk", "cross"), None),
        P(("blk", "cross"), None),
        P(("blk", "cross")),
        P(("blk", "cross"), None),
        P(None, ("blk", "cross"), None),
        P(("blk", "cross"), None),
        P(("blk", "cross")),
        P(),
        P(),
    )
    return jax.shard_map(
        shards,
        mesh=mesh,
        in_specs=placed,
        out_specs=(P("blk", "cross", None), P(("blk", "cross"), None)),
        check_vma=False,
    )
```

```python
import jax
import jax.numpy as jnp
from jax import lax
from jax.experimental import pallas as pl
from jax.experimental.pallas import tpu as pltpu
from jax.sharding import PartitionSpec as P

CX = 8
CY = 64
NZ = 1024
BPH = 8
NODES = 128
PT = 128
BT = 256
FT = 896
GROUPS = FT // 4
SLOTS = 4
GX = CX + 1
GY = CY + 1
AXES = ("blk", "cross")
PARTS = 4
ZL = 16
LINE = SLOTS * 1024 + 128
VMEM_BYTES = 62 * 1024 * 1024
ALL_VMEM = 63 * 1024 * 1024 + 512 * 1024
HALF_VMEM = 32 * 1024 * 1024
f32 = jnp.float32
bf16 = jnp.bfloat16
i32 = jnp.int32


def shifted(value, axis, steps):
    count = lax.axis_size(axis)
    pairs = [(source, (source + steps) % count) for source in range(count)]
    return lax.ppermute(value, axis, pairs)


def diagonal(value):
    blocks, columns = lax.axis_size("blk"), lax.axis_size("cross")
    pairs = [
        (b * columns + c, (b + 1) % blocks * columns + (c + 1) % columns)
        for b in range(blocks)
        for c in range(columns)
    ]
    return lax.ppermute(value, AXES, pairs)


def iota(shape, dim):
    return lax.broadcasted_iota(i32, shape, dim)


def two_terms(value):
    high = value.astype(bf16).astype(f32)
    return high, value - high


def nt_dot(left, right):
    return lax.dot_general(left, right, (((1,), (1,)), ((), ())), preferred_element_type=f32)


def corner_weights(u, v, w, m):
    result = []
    for part_x in (1.0 - u, u):
        row = []
        for part_y in (1.0 - v, v):
            plane = m * part_x * part_y
            row.append((plane * (1.0 - w), plane * w))
        result.append(row)
    return result


def fine_profile_kernel(
    box_ref, boxes_ref, columns_ref, zbin_ref, frac_ref, mass_ref, out_ref, label_ref, head_ref, last_ref
):
    part = pl.program_id(0)

    @pl.when(part == 0)
    def _():
        out_ref[...] = jnp.zeros(out_ref.shape, f32)
        boxes = boxes_ref[...]
        columns = columns_ref[...]
        x = (columns * 4370) >> 16
        y = columns - x * 15
        label_ref[...] = ((y & 1) * 1024 + (x * 8 + (y >> 1)) * 8 + (boxes & 7)).astype(f32)
        head_ref[...] = jnp.zeros((1, 128), f32)
        last_ref[0] = -1

    four_lanes = iota((1, 128), 1) // 4
    sub = iota((8, PT), 0)
    turn = (iota((8, PT), 1) // ZL + sub) & 7
    z_row = iota((ZL, PT), 0).astype(f32).astype(bf16)
    one = jnp.ones((ZL, PT), bf16)
    zero = jnp.zeros((ZL, PT), bf16)
    none = jnp.zeros((16, PT), bf16)
    uppers = 64 // ZL

    def step(i, carry):
        last, head = carry
        rows = pl.ds(pl.multiple_of(i * 8, 8), 8)
        z = zbin_ref[rows, :]
        weights = corner_weights(frac_ref[0, rows, :], frac_ref[1, rows, :], frac_ref[2, rows, :], mass_ref[rows, :])
        left = []
        right = []
        for e in (0, 1):
            cell = z + e
            upper = (cell // ZL).astype(f32)
            upper = jnp.concatenate([upper, upper], axis=0).astype(bf16)
            masks = [upper == none + h for h in range(uppers)]
            parts = []
            for a in (0, 1):
                for b in (0, 1):
                    terms = jnp.concatenate(two_terms(weights[a][b][e]), axis=0).astype(bf16)
                    for mask in masks:
                        parts.append(jnp.where(mask, terms, none))
            left.append(jnp.concatenate(parts, axis=0))
            lower = (cell & (ZL - 1)).astype(f32)
            hots = []
            for t in reversed(range(8)):
                row = jnp.broadcast_to(lower[t:t + 1, :], (ZL, PT)).astype(bf16)
                hots.append(jnp.where(row == z_row, one, zero))
            right.append(jnp.concatenate(hots, axis=0))
        product = nt_dot(jnp.concatenate(left, axis=1), jnp.concatenate(right, axis=1))
        halves = []
        for a in (0, 1):
            gathered = None
            for q in range(2 * uppers):
                start = (2 * uppers * a + q) * 16
                total = product[start:start + 8, :] + product[start + 8:start + 16, :]
                value = pltpu.roll(total, ZL * (q + 1), 1) if q < 7 else total
                gathered = value if gathered is None else jnp.where(turn == q, value, gathered)
            halves.append(pltpu.roll(gathered, 0, 1, stride=ZL, stride_axis=0))
        first = jnp.where(sub < 4, halves[0], pltpu.roll(halves[1], 4, 0))
        second = jnp.where(sub < 4, pltpu.roll(halves[0], 4, 0), halves[1])
        for g, value in ((0, first), (1, second)):
            group = part * (FT // PARTS // 4) + i * 2 + g
            owner = box_ref[group * 4] >> 3
            out_ref[owner, :, pl.ds(pl.multiple_of((group & 3) * 1024, 1024), 1024)] = value.reshape(1, 1024)
            label = jnp.where(four_lanes == (group & 31), label_ref[pl.ds(group >> 5, 1), :], 0.0)
            head = jnp.where(owner == last, head, 0.0) + label
            last = owner
            out_ref[owner, :, 4096:4224] = head
        return last, head

    steps = FT // PARTS // 8
    last, head = lax.fori_loop(0, steps, step, (last_ref[0], head_ref[...]), unroll=steps)
    last_ref[0] = last
    head_ref[...] = head


def fine_profiles(tile_box, fine_column, fine_zbin, fine_frac, fine_weight):
    tiles = FT // PARTS
    return pl.pallas_call(
        fine_profile_kernel,
        out_shape=jax.ShapeDtypeStruct((NODES, 1, LINE), f32),
        grid=(PARTS,),
        in_specs=[
            pl.BlockSpec(memory_space=pltpu.SMEM),
            pl.BlockSpec((FT // 128, 128), lambda i: (0, 0)),
            pl.BlockSpec((FT // 128, 128), lambda i: (0, 0)),
            pl.BlockSpec((tiles, PT), lambda i: (i, 0)),
            pl.BlockSpec((3, tiles, PT), lambda i: (0, i, 0)),
            pl.BlockSpec((tiles, PT), lambda i: (i, 0)),
        ],
        out_specs=pl.BlockSpec((NODES, 1, LINE), lambda i: (0, 0, 0)),
        scratch_shapes=[
            pltpu.VMEM((FT // 128, 128), f32),
            pltpu.VMEM((1, 128), f32),
            pltpu.SMEM((1,), i32),
        ],
        compiler_params=pltpu.CompilerParams(vmem_limit_bytes=VMEM_BYTES),
        cost_estimate=pl.CostEstimate(flops=2 * 128 * 256 * 256 * 112, bytes_accessed=4500000, transcendentals=0),
        name="fine_profiles",
    )(
        tile_box,
        tile_box.reshape(FT // 128, 128),
        fine_column.reshape(FT // 128, 128),
        fine_zbin,
        fine_frac,
        fine_weight,
    )


def tables_kernel(me_ref, home_ref, anchor_ref, owner_ref, place_ref):
    index = iota((8, 128), 0) * 128 + iota((8, 128), 1)
    left = jnp.where(home_ref[...] == me_ref[0], index, NODES * BPH)
    for n in range(BPH):
        box = jnp.minimum(jnp.min(left), NODES * BPH - 1)
        left = jnp.where(left == box, NODES * BPH, left)
        owner_ref[n] = box >> 3
        place_ref[n] = anchor_ref[box]


def tables(me, box_home, box_anchor):
    smem = pl.BlockSpec(memory_space=pltpu.SMEM)
    return pl.pallas_call(
        tables_kernel,
        out_shape=(jax.ShapeDtypeStruct((BPH,), i32), jax.ShapeDtypeStruct((BPH,), i32)),
        in_specs=[smem, pl.BlockSpec(memory_space=pltpu.VMEM), smem],
        out_specs=(smem, smem),
        cost_estimate=pl.CostEstimate(flops=4000000, bytes_accessed=40000, transcendentals=0),
        name="tables",
    )(me, box_home.reshape(8, 128), box_anchor)


def base_kernel(column_ref, zbin_ref, frac_ref, mass_ref, core_ref, front_ref, side_ref, corner_ref, grid_ref):
    grid_ref[...] = jnp.zeros(grid_ref.shape, f32)
    upper_row = iota((8, PT), 0)
    lower_row = iota((128, PT), 0)

    def step(i, carry):
        rows = pl.ds(pl.multiple_of(i * 8, 8), 8)
        z = zbin_ref[rows, :]
        weights = corner_weights(frac_ref[0, rows, :], frac_ref[1, rows, :], frac_ref[2, rows, :], mass_ref[rows, :])
        cells = (z, (z + 1) & (NZ - 1))
        uppers = [cell >> 7 for cell in cells]
        lowers = [cell & 127 for cell in cells]
        for t in range(8):
            left = []
            right = []
            for e in (0, 1):
                mask = jnp.broadcast_to(uppers[e][t:t + 1, :], (8, PT)) == upper_row
                parts = []
                for a in (0, 1):
                    for b in (0, 1):
                        row = jnp.broadcast_to(weights[a][b][e][t:t + 1, :], (8, PT))
                        parts.extend(two_terms(jnp.where(mask, row, 0.0)))
                left.append(jnp.concatenate(parts, axis=0).astype(bf16))
                low = jnp.broadcast_to(lowers[e][t:t + 1, :], (128, PT))
                right.append(jnp.where(low == lower_row, 1.0, 0.0).astype(bf16))
            product = nt_dot(jnp.concatenate(left, axis=1), jnp.concatenate(right, axis=1))
            q = column_ref[i * 8 + t]
            corner = (q // CY) * GY + q % CY
            for a in (0, 1):
                for b in (0, 1):
                    start = (2 * a + b) * 16
                    place = pl.ds(pl.multiple_of((corner + a * GY + b) * 8, 8), 8)
                    grid_ref[place, :] += product[start:start + 8, :] + product[start + 8:start + 16, :]
        return carry

    lax.fori_loop(0, BT // 8, step, 0, unroll=2)
    for x in range(GX):
        for band in range(CY // 8):
            for part in range(8):
                rows = grid_ref[pl.ds((x * GY + band * 8) * 8 + part, 8, stride=8), :]
                if x < CX:
                    core_ref[x, band * 8:band * 8 + 8, part * 128:part * 128 + 128] = rows
                else:
                    front_ref[band * 8:band * 8 + 8, part * 128:part * 128 + 128] = rows
    for part in range(8):
        lanes = slice(part * 128, part * 128 + 128)
        side_ref[:, lanes] = grid_ref[pl.ds(CY * 8 + part, 8, stride=GY * 8), :]
        corner_row = (CX * GY + CY) * 8 + part
        corner_ref[0:1, lanes] = grid_ref[corner_row:corner_row + 1, :]


def base_deposit(base_column, base_zbin, base_frac, base_weight):
    vmem = pl.BlockSpec(memory_space=pltpu.VMEM)
    return pl.pallas_call(
        base_kernel,
        out_shape=(
            jax.ShapeDtypeStruct((CX, CY, NZ), f32),
            jax.ShapeDtypeStruct((CY, NZ), f32),
            jax.ShapeDtypeStruct((CX, NZ), f32),
            jax.ShapeDtypeStruct((1, NZ), f32),
        ),
        in_specs=[pl.BlockSpec(memory_space=pltpu.SMEM), vmem, vmem, vmem],
        out_specs=(vmem, vmem, vmem, vmem),
        scratch_shapes=[pltpu.VMEM((GX * GY * 8, 128), f32)],
        compiler_params=pltpu.CompilerParams(vmem_limit_bytes=HALF_VMEM),
        cost_estimate=pl.CostEstimate(flops=10000000000, bytes_accessed=5000000, transcendentals=0),
        name="base_deposit",
    )(base_column, base_zbin, base_frac, base_weight)


def halo_kernel(core_ref, front_ref, side_ref, corner_ref, out_ref, face_ref, band_ref, sem):
    slab = pltpu.make_async_copy(core_ref.at[0], face_ref, sem.at[0])
    band = pltpu.make_async_copy(core_ref.at[pl.ds(1, CX - 1), pl.ds(0, 8), :], band_ref, sem.at[1])
    slab.start()
    band.start()
    slab.wait()
    face_ref[...] += front_ref[...]
    face_ref[0:1, :] += side_ref[0:1, :] + corner_ref[...]
    slab_out = pltpu.make_async_copy(face_ref, out_ref.at[0], sem.at[2])
    slab_out.start()
    band.wait()
    for x in range(1, CX):
        band_ref[x - 1, 0:1, :] += side_ref[x:x + 1, :]
    band_out = pltpu.make_async_copy(band_ref, out_ref.at[pl.ds(1, CX - 1), pl.ds(0, 8), :], sem.at[3])
    band_out.start()
    slab_out.wait()
    band_out.wait()


def halo_add(core, front, side, corner):
    vmem = pl.BlockSpec(memory_space=pltpu.VMEM)
    hbm = pl.BlockSpec(memory_space=pltpu.HBM)
    return pl.pallas_call(
        halo_kernel,
        out_shape=jax.ShapeDtypeStruct((CX, CY, NZ), f32),
        in_specs=[hbm, vmem, vmem, vmem],
        out_specs=hbm,
        input_output_aliases={0: 0},
        scratch_shapes=[
            pltpu.VMEM((CY, NZ), f32),
            pltpu.VMEM((CX - 1, 8, NZ), f32),
            pltpu.SemaphoreType.DMA((4,)),
        ],
        compiler_params=pltpu.CompilerParams(vmem_limit_bytes=HALF_VMEM),
        cost_estimate=pl.CostEstimate(flops=1000000, bytes_accessed=1500000, transcendentals=0),
        name="halo_add",
    )(core, front, side, corner)


ROWS = NODES * SLOTS * 8
MB = 256


def arrival_rows(heads):
    count = heads.shape[0]
    line = iota((128, 128), 0)
    lane = iota((128, 128), 1)
    spread = jnp.where(line % 16 == (lane // 8) % 4 * 4 + lane % 4, 1.0, 0.0).astype(bf16)
    labels = (heads + 0.5).astype(i32)
    digits = jnp.concatenate([(labels >> 4).astype(f32), (labels & 15).astype(f32)], axis=0).astype(bf16)
    wide = jnp.dot(digits, spread, preferred_element_type=f32)
    wide = wide[0:count, :] * 16.0 + wide[count:2 * count, :]
    wide = jnp.where(iota((count, 128), 0) % 4 == iota((count, 128), 1) // 32, wide, 0.0)
    shift = 64 * ((iota((1, 128), 1) // 4) % 2)
    return [
        (jnp.sum(wide[4 * k:4 * k + 4, :], axis=0, keepdims=True) + 0.5).astype(i32) + shift
        for k in range(count // 4)
    ]


def one_hot(lines, target):
    one = jnp.ones(target.shape, bf16)
    zero = jnp.zeros(target.shape, bf16)
    return jnp.concatenate(
        [jnp.where(jnp.broadcast_to(line, target.shape).astype(jnp.int16) == target, one, zero) for line in lines],
        axis=1,
    )


def arrival_terms(got_ref, first, count):
    parts = [got_ref[s, :, 0:SLOTS * 1024].reshape(SLOTS * 8, 128) for s in range(first, first + count)]
    high, low = two_terms(jnp.concatenate(parts, axis=0))
    return jnp.concatenate([high.astype(bf16), low.astype(bf16)], axis=1)


def coarse_kernel(home_ref, got_ref, send_ref, head_ref, sums_ref, part_ref, sem):
    terms = arrival_terms(got_ref, 0, NODES)
    lines = []
    for k, row in enumerate(arrival_rows(got_ref[:, 0, SLOTS * 1024:LINE])):
        head_ref[k:k + 1, :] = row
        lines.append((row >> 10) * 512 + ((row >> 7) & 7) * 64 + (row & 63))
    for m in range(1024 // MB):
        target = (iota((MB, 128), 0) + m * MB).astype(jnp.int16)
        product = jnp.dot(one_hot(lines, target), terms, preferred_element_type=f32)
        sums_ref[m * MB:(m + 1) * MB, :] = product[:, 0:128] + product[:, 128:256]
    lane = iota((64, 128), 1)
    fold_row = iota((512, 128), 0)
    fold_lane = iota((512, 128), 1)
    fold = jnp.where((fold_row // 128) * 32 + (fold_row % 64) // 2 == fold_lane, 1.0, 0.0).astype(bf16)
    for far in (0, 1):
        pieces = []
        for q in range(4):
            spot = (4 * far + q) * 64
            odd = sums_ref[512 + spot:512 + spot + 64, :]
            before = jnp.concatenate([jnp.zeros((8, 128), f32), odd[0:56, :]], axis=0)
            both = sums_ref[spot:spot + 64, :] + jnp.where(lane < 64, odd, before)
            pieces.append(jnp.concatenate(two_terms(both), axis=0).astype(bf16))
        folded = jnp.dot(jnp.concatenate(pieces, axis=1), fold, preferred_element_type=f32)
        part_ref[far * 64:far * 64 + 64, :] = folded[0:64, :] + folded[64:128, :]
    copies = []
    for box in range(BPH):
        for far in (0, 1):
            hot = part_ref[pl.ds(far * 64 + box, 8, stride=8), :]
            part_ref[128 + box * 16 + far * 8:128 + box * 16 + far * 8 + 8, :] = hot
    for box in range(BPH):
        copy = pltpu.make_async_copy(
            part_ref.at[pl.ds(128 + box * 16, 16), :], send_ref.at[home_ref[box]], sem.at[box]
        )
        copy.start()
        copies.append(copy)
    for copy in copies:
        copy.wait()


def coarse_deposit(homes, arrived):
    hbm = pl.BlockSpec(memory_space=pltpu.HBM)
    return pl.pallas_call(
        coarse_kernel,
        out_shape=(jax.ShapeDtypeStruct((NODES, 16, 128), f32), jax.ShapeDtypeStruct((32, 128), i32)),
        in_specs=[pl.BlockSpec(memory_space=pltpu.SMEM), pl.BlockSpec(memory_space=pltpu.VMEM)],
        out_specs=(hbm, pl.BlockSpec(memory_space=pltpu.VMEM)),
        scratch_shapes=[
            pltpu.VMEM((1024, 128), f32),
            pltpu.VMEM((256, 128), f32),
            pltpu.SemaphoreType.DMA((BPH,)),
        ],
        compiler_params=pltpu.CompilerParams(vmem_limit_bytes=HALF_VMEM),
        cost_estimate=pl.CostEstimate(flops=1000, bytes_accessed=1000, transcendentals=0),
        name="coarse_deposit",
    )(homes, arrived)


def fine_kernel(head_ref, got_ref, fine_ref, terms_ref, sums_ref, hot_ref):
    terms_ref[...] = arrival_terms(got_ref, 0, NODES)

    def block(m, carry):
        target = (iota((MB, 128), 0) + m * MB).astype(jnp.int16)
        hot_ref[...] = one_hot([head_ref[k:k + 1, :] for k in range(ROWS // 128)], target)
        product = jnp.dot(hot_ref[...], terms_ref[...], preferred_element_type=f32)
        sums_ref[pl.ds(pl.multiple_of(m * MB, MB), MB), :] = product[:, 0:128] + product[:, 128:256]
        return carry

    lax.fori_loop(0, 2048 // MB, block, 0)
    lane = iota((8, 128), 1)
    for x in range(16):
        for y in range(8):
            spot = (x * 8 + y) * 8
            odd = sums_ref[1024 + spot:1024 + spot + 8, :]
            before = sums_ref[1024 + spot - 8:1024 + spot, :] if y else jnp.zeros((8, 128), f32)
            cross = pltpu.roll(jnp.where(lane < 64, odd, before), 64, 1)
            fine_ref[:, spot * 16:spot * 16 + 128] = sums_ref[spot:spot + 8, :] + cross


def fine_deposit(header, arrived):
    vmem = pl.BlockSpec(memory_space=pltpu.VMEM)
    return pl.pallas_call(
        fine_kernel,
        out_shape=jax.ShapeDtypeStruct((BPH, 16384), f32),
        in_specs=[vmem, vmem],
        out_specs=vmem,
        scratch_shapes=[
            pltpu.VMEM((ROWS, 256), bf16),
            pltpu.VMEM((2048, 128), f32),
            pltpu.VMEM((MB, ROWS), bf16),
        ],
        compiler_params=pltpu.CompilerParams(vmem_limit_bytes=HALF_VMEM),
        cost_estimate=pl.CostEstimate(flops=2 * 2048 * ROWS * 256, bytes_accessed=4000000, transcendentals=0),
        name="fine_deposit",
    )(header, arrived)


def lattice_kernel(owner_ref, place_ref, base_ref, got_ref, out_ref, held_ref, block_ref, got_sem, in_sem, out_sem):
    def spot_of(n, grid):
        place = place_ref[n]
        rows = pl.ds(pl.multiple_of(((place >> 5) & 7) * 8, 8), 8)
        lanes = pl.ds(pl.multiple_of(((place >> 2) & 7) * 128, 128), 128)
        return grid.at[:, rows, lanes]

    copies = []
    for n in range(BPH):
        copies.append(pltpu.make_async_copy(got_ref.at[owner_ref[n]], held_ref.at[n], got_sem.at[n]))
        copies.append(pltpu.make_async_copy(spot_of(n, base_ref), block_ref.at[n], in_sem.at[n]))
    for copy in copies:
        copy.start()
    firsts = []
    for n in range(BPH):
        first = jnp.int32(n)
        for k in reversed(range(n)):
            first = jnp.where(place_ref[k] >> 2 == place_ref[n] >> 2, k, first)
        firsts.append(first)
    for copy in copies:
        copy.wait()
    quarter = iota((8, 128), 1) // 32
    for n in range(BPH):
        spot = place_ref[n] & 3
        for x in range(CX):
            value = held_ref[n, (x // 4) * 8:(x // 4) * 8 + 8, :]
            moved = pltpu.roll(value, ((spot - x % 4 + 4) & 3) * 32, 1)
            block_ref[firsts[n], x] += jnp.where(quarter == spot, moved, 0.0)
    for n in range(BPH):
        @pl.when(firsts[n] == n)
        def _():
            pltpu.make_async_copy(block_ref.at[n], spot_of(n, out_ref), out_sem.at[n]).start()
    for n in range(BPH):
        @pl.when(firsts[n] == n)
        def _():
            pltpu.make_async_copy(block_ref.at[n], spot_of(n, out_ref), out_sem.at[n]).wait()


def lattice_add(owners, places, base, arrived):
    smem = pl.BlockSpec(memory_space=pltpu.SMEM)
    hbm = pl.BlockSpec(memory_space=pltpu.HBM)
    return pl.pallas_call(
        lattice_kernel,
        out_shape=jax.ShapeDtypeStruct((CX, CY, NZ), f32),
        in_specs=[smem, smem, hbm, hbm],
        out_specs=hbm,
        input_output_aliases={2: 0},
        scratch_shapes=[
            pltpu.VMEM((BPH, 16, 128), f32),
            pltpu.VMEM((BPH, CX, 8, 128), f32),
            pltpu.SemaphoreType.DMA((BPH,)),
            pltpu.SemaphoreType.DMA((BPH,)),
            pltpu.SemaphoreType.DMA((BPH,)),
        ],
        compiler_params=pltpu.CompilerParams(vmem_limit_bytes=ALL_VMEM),
        cost_estimate=pl.CostEstimate(flops=1000000, bytes_accessed=1000000, transcendentals=0),
        name="lattice_add",
    )(owners, places, base, arrived)


def shards(
    base_column,
    base_zbin,
    base_frac,
    base_weight,
    fine_column,
    fine_zbin,
    fine_frac,
    fine_weight,
    tile_box,
    box_home,
    box_anchor,
):
    myself = lax.axis_index(AXES).astype(i32)
    homes = lax.dynamic_slice_in_dim(box_home, myself * BPH, BPH, 0)
    outgoing = fine_profiles(tile_box, fine_column, fine_zbin, fine_frac, fine_weight)
    outgoing, base_column, myself = lax.optimization_barrier((outgoing, base_column, myself))
    arrived = lax.all_to_all(outgoing, AXES, split_axis=0, concat_axis=0, tiled=True)
    owners, places = tables(myself.reshape(1), box_home, box_anchor)
    core, front, side, corner = base_deposit(base_column, base_zbin, base_frac, base_weight)
    outer = (shifted(front, "blk", 1), shifted(side, "cross", 1), diagonal(corner))
    arrived, core, owners, places = lax.optimization_barrier((arrived, core, owners, places))
    sending, header = coarse_deposit(homes, arrived)
    sending, header, front, side, corner = lax.optimization_barrier((sending, header, *outer))
    returned = lax.all_to_all(sending, AXES, split_axis=0, concat_axis=0, tiled=True)
    fine_rows = fine_deposit(header, arrived)
    base = halo_add(core, front, side, corner)
    returned, base, fine_rows = lax.optimization_barrier((returned, base, fine_rows))
    base_out = lattice_add(owners, places, base, returned)
    return (base_out, fine_rows)


def solution(mesh):
    placed = (
        P(("blk", "cross")),
        P(("blk", "cross"), None),
        P(None, ("blk", "cross"), None),
        P(("blk", "cross"), None),
        P(("blk", "cross")),
        P(("blk", "cross"), None),
        P(None, ("blk", "cross"), None),
        P(("blk", "cross"), None),
        P(("blk", "cross")),
        P(),
        P(),
    )
    return jax.shard_map(
        shards,
        mesh=mesh,
        in_specs=placed,
        out_specs=(P("blk", "cross", None), P(("blk", "cross"), None)),
        check_vma=False,
    )
```

```python
import jax
import jax.numpy as jnp
from jax import lax
from jax.experimental import pallas as pl
from jax.experimental.pallas import tpu as pltpu
from jax.sharding import PartitionSpec as P

CX = 8
CY = 64
NZ = 1024
BPH = 8
NODES = 128
PT = 128
BT = 256
FT = 896
GROUPS = FT // 4
SLOTS = 4
GX = CX + 1
GY = CY + 1
AXES = ("blk", "cross")
PARTS = 4
ZL = 16
CHUNKS = 8
LINE = SLOTS * 1024 + 128
VMEM_BYTES = 62 * 1024 * 1024
ALL_VMEM = 63 * 1024 * 1024 + 512 * 1024
HALF_VMEM = 32 * 1024 * 1024
f32 = jnp.float32
bf16 = jnp.bfloat16
i32 = jnp.int32


def shifted(value, axis, steps):
    count = lax.axis_size(axis)
    pairs = [(source, (source + steps) % count) for source in range(count)]
    return lax.ppermute(value, axis, pairs)


def diagonal(value):
    blocks, columns = lax.axis_size("blk"), lax.axis_size("cross")
    pairs = [
        (b * columns + c, (b + 1) % blocks * columns + (c + 1) % columns)
        for b in range(blocks)
        for c in range(columns)
    ]
    return lax.ppermute(value, AXES, pairs)


def iota(shape, dim):
    return lax.broadcasted_iota(i32, shape, dim)


def two_terms(value):
    high = value.astype(bf16).astype(f32)
    return high, value - high


def nt_dot(left, right):
    return lax.dot_general(left, right, (((1,), (1,)), ((), ())), preferred_element_type=f32)


def corner_weights(u, v, w, m):
    result = []
    for part_x in (1.0 - u, u):
        row = []
        for part_y in (1.0 - v, v):
            plane = m * part_x * part_y
            row.append((plane * (1.0 - w), plane * w))
        result.append(row)
    return result


def fine_profile_kernel(
    box_ref, boxes_ref, columns_ref, zbin_ref, frac_ref, mass_ref, send_ref, out_ref, label_ref, head_ref, last_ref, sem
):
    part = pl.program_id(0)

    @pl.when(part == 0)
    def _():
        out_ref[...] = jnp.zeros(out_ref.shape, f32)
        boxes = boxes_ref[...]
        columns = columns_ref[...]
        x = (columns * 4370) >> 16
        y = columns - x * 15
        label_ref[...] = ((y & 1) * 1024 + (x * 8 + (y >> 1)) * 8 + (boxes & 7)).astype(f32)
        head_ref[...] = jnp.zeros((1, 128), f32)
        last_ref[0] = -1
        last_ref[1] = 0

    four_lanes = iota((1, 128), 1) // 4
    sub = iota((8, PT), 0)
    turn = (iota((8, PT), 1) // ZL + sub) & 7
    z_row = iota((ZL, PT), 0).astype(f32).astype(bf16)
    one = jnp.ones((ZL, PT), bf16)
    zero = jnp.zeros((ZL, PT), bf16)
    none = jnp.zeros((16, PT), bf16)
    uppers = 64 // ZL

    def step(i, carry):
        last, head = carry
        rows = pl.ds(pl.multiple_of(i * 8, 8), 8)
        z = zbin_ref[rows, :]
        weights = corner_weights(frac_ref[0, rows, :], frac_ref[1, rows, :], frac_ref[2, rows, :], mass_ref[rows, :])
        left = []
        right = []
        for e in (0, 1):
            cell = z + e
            upper = (cell // ZL).astype(f32)
            upper = jnp.concatenate([upper, upper], axis=0).astype(bf16)
            masks = [upper == none + h for h in range(uppers)]
            parts = []
            for a in (0, 1):
                for b in (0, 1):
                    terms = jnp.concatenate(two_terms(weights[a][b][e]), axis=0).astype(bf16)
                    for mask in masks:
                        parts.append(jnp.where(mask, terms, none))
            left.append(jnp.concatenate(parts, axis=0))
            lower = (cell & (ZL - 1)).astype(f32)
            hots = []
            for t in reversed(range(8)):
                row = jnp.broadcast_to(lower[t:t + 1, :], (ZL, PT)).astype(bf16)
                hots.append(jnp.where(row == z_row, one, zero))
            right.append(jnp.concatenate(hots, axis=0))
        product = nt_dot(jnp.concatenate(left, axis=1), jnp.concatenate(right, axis=1))
        halves = []
        for a in (0, 1):
            gathered = None
            for q in range(2 * uppers):
                start = (2 * uppers * a + q) * 16
                total = product[start:start + 8, :] + product[start + 8:start + 16, :]
                value = pltpu.roll(total, ZL * (q + 1), 1) if q < 7 else total
                gathered = value if gathered is None else jnp.where(turn == q, value, gathered)
            halves.append(pltpu.roll(gathered, 0, 1, stride=ZL, stride_axis=0))
        first = jnp.where(sub < 4, halves[0], pltpu.roll(halves[1], 4, 0))
        second = jnp.where(sub < 4, pltpu.roll(halves[0], 4, 0), halves[1])
        for g, value in ((0, first), (1, second)):
            group = part * (FT // PARTS // 4) + i * 2 + g
            owner = box_ref[group * 4] >> 3
            out_ref[owner, :, pl.ds(pl.multiple_of((group & 3) * 1024, 1024), 1024)] = value.reshape(1, 1024)
            label = jnp.where(four_lanes == (group & 31), label_ref[pl.ds(group >> 5, 1), :], 0.0)
            head = jnp.where(owner == last, head, 0.0) + label
            last = owner
            out_ref[owner, :, 4096:4224] = head
        return last, head

    steps = FT // PARTS // 8
    last, head = lax.fori_loop(0, steps, step, (last_ref[0], head_ref[...]), unroll=steps)
    last_ref[0] = last
    head_ref[...] = head
    span = NODES // CHUNKS
    copies = [
        pltpu.make_async_copy(out_ref.at[pl.ds(c * span, span)], send_ref.at[pl.ds(c * span, span)], sem.at[c])
        for c in range(CHUNKS)
    ]
    sent = last_ref[1]
    ready = jnp.where(part == PARTS - 1, CHUNKS, last // span)
    for c in range(CHUNKS):
        @pl.when((c >= sent) & (c < ready))
        def _():
            copies[c].start()
    last_ref[1] = ready

    @pl.when(part == PARTS - 1)
    def _():
        for copy in copies:
            copy.wait()


def fine_profiles(tile_box, fine_column, fine_zbin, fine_frac, fine_weight):
    tiles = FT // PARTS
    return pl.pallas_call(
        fine_profile_kernel,
        out_shape=jax.ShapeDtypeStruct((NODES, 1, LINE), f32),
        grid=(PARTS,),
        in_specs=[
            pl.BlockSpec(memory_space=pltpu.SMEM),
            pl.BlockSpec((FT // 128, 128), lambda i: (0, 0)),
            pl.BlockSpec((FT // 128, 128), lambda i: (0, 0)),
            pl.BlockSpec((tiles, PT), lambda i: (i, 0)),
            pl.BlockSpec((3, tiles, PT), lambda i: (0, i, 0)),
            pl.BlockSpec((tiles, PT), lambda i: (i, 0)),
        ],
        out_specs=pl.BlockSpec(memory_space=pltpu.HBM),
        scratch_shapes=[
            pltpu.VMEM((NODES, 1, LINE), f32),
            pltpu.VMEM((FT // 128, 128), f32),
            pltpu.VMEM((1, 128), f32),
            pltpu.SMEM((2,), i32),
            pltpu.SemaphoreType.DMA((CHUNKS,)),
        ],
        compiler_params=pltpu.CompilerParams(vmem_limit_bytes=VMEM_BYTES),
        cost_estimate=pl.CostEstimate(flops=2 * 128 * 256 * 256 * 112, bytes_accessed=4500000, transcendentals=0),
        name="fine_profiles",
    )(
        tile_box,
        tile_box.reshape(FT // 128, 128),
        fine_column.reshape(FT // 128, 128),
        fine_zbin,
        fine_frac,
        fine_weight,
    )


def tables_kernel(me_ref, home_ref, anchor_ref, owner_ref, place_ref):
    index = iota((8, 128), 0) * 128 + iota((8, 128), 1)
    left = jnp.where(home_ref[...] == me_ref[0], index, NODES * BPH)
    for n in range(BPH):
        box = jnp.minimum(jnp.min(left), NODES * BPH - 1)
        left = jnp.where(left == box, NODES * BPH, left)
        owner_ref[n] = box >> 3
        place_ref[n] = anchor_ref[box]


def tables(me, box_home, box_anchor):
    smem = pl.BlockSpec(memory_space=pltpu.SMEM)
    return pl.pallas_call(
        tables_kernel,
        out_shape=(jax.ShapeDtypeStruct((BPH,), i32), jax.ShapeDtypeStruct((BPH,), i32)),
        in_specs=[smem, pl.BlockSpec(memory_space=pltpu.VMEM), smem],
        out_specs=(smem, smem),
        cost_estimate=pl.CostEstimate(flops=4000000, bytes_accessed=40000, transcendentals=0),
        name="tables",
    )(me, box_home.reshape(8, 128), box_anchor)


def base_kernel(column_ref, zbin_ref, frac_ref, mass_ref, core_ref, front_ref, side_ref, corner_ref, grid_ref):
    grid_ref[...] = jnp.zeros(grid_ref.shape, f32)
    upper_row = iota((8, PT), 0)
    lower_row = iota((128, PT), 0)

    def step(i, carry):
        rows = pl.ds(pl.multiple_of(i * 8, 8), 8)
        z = zbin_ref[rows, :]
        weights = corner_weights(frac_ref[0, rows, :], frac_ref[1, rows, :], frac_ref[2, rows, :], mass_ref[rows, :])
        cells = (z, (z + 1) & (NZ - 1))
        uppers = [cell >> 7 for cell in cells]
        lowers = [cell & 127 for cell in cells]
        for t in range(8):
            left = []
            right = []
            for e in (0, 1):
                mask = jnp.broadcast_to(uppers[e][t:t + 1, :], (8, PT)) == upper_row
                parts = []
                for a in (0, 1):
                    for b in (0, 1):
                        row = jnp.broadcast_to(weights[a][b][e][t:t + 1, :], (8, PT))
                        parts.extend(two_terms(jnp.where(mask, row, 0.0)))
                left.append(jnp.concatenate(parts, axis=0).astype(bf16))
                low = jnp.broadcast_to(lowers[e][t:t + 1, :], (128, PT))
                right.append(jnp.where(low == lower_row, 1.0, 0.0).astype(bf16))
            product = nt_dot(jnp.concatenate(left, axis=1), jnp.concatenate(right, axis=1))
            q = column_ref[i * 8 + t]
            corner = (q // CY) * GY + q % CY
            for a in (0, 1):
                for b in (0, 1):
                    start = (2 * a + b) * 16
                    place = pl.ds(pl.multiple_of((corner + a * GY + b) * 8, 8), 8)
                    grid_ref[place, :] += product[start:start + 8, :] + product[start + 8:start + 16, :]
        return carry

    lax.fori_loop(0, BT // 8, step, 0, unroll=2)
    for x in range(GX):
        for band in range(CY // 8):
            for part in range(8):
                rows = grid_ref[pl.ds((x * GY + band * 8) * 8 + part, 8, stride=8), :]
                if x < CX:
                    core_ref[x, band * 8:band * 8 + 8, part * 128:part * 128 + 128] = rows
                else:
                    front_ref[band * 8:band * 8 + 8, part * 128:part * 128 + 128] = rows
    for part in range(8):
        lanes = slice(part * 128, part * 128 + 128)
        side_ref[:, lanes] = grid_ref[pl.ds(CY * 8 + part, 8, stride=GY * 8), :]
        corner_row = (CX * GY + CY) * 8 + part
        corner_ref[0:1, lanes] = grid_ref[corner_row:corner_row + 1, :]


def base_deposit(base_column, base_zbin, base_frac, base_weight):
    vmem = pl.BlockSpec(memory_space=pltpu.VMEM)
    return pl.pallas_call(
        base_kernel,
        out_shape=(
            jax.ShapeDtypeStruct((CX, CY, NZ), f32),
            jax.ShapeDtypeStruct((CY, NZ), f32),
            jax.ShapeDtypeStruct((CX, NZ), f32),
            jax.ShapeDtypeStruct((1, NZ), f32),
        ),
        in_specs=[pl.BlockSpec(memory_space=pltpu.SMEM), vmem, vmem, vmem],
        out_specs=(vmem, vmem, vmem, vmem),
        scratch_shapes=[pltpu.VMEM((GX * GY * 8, 128), f32)],
        compiler_params=pltpu.CompilerParams(vmem_limit_bytes=HALF_VMEM),
        cost_estimate=pl.CostEstimate(flops=10000000000, bytes_accessed=5000000, transcendentals=0),
        name="base_deposit",
    )(base_column, base_zbin, base_frac, base_weight)


def halo_kernel(core_ref, front_ref, side_ref, corner_ref, out_ref, face_ref, band_ref, sem):
    slab = pltpu.make_async_copy(core_ref.at[0], face_ref, sem.at[0])
    band = pltpu.make_async_copy(core_ref.at[pl.ds(1, CX - 1), pl.ds(0, 8), :], band_ref, sem.at[1])
    slab.start()
    band.start()
    slab.wait()
    face_ref[...] += front_ref[...]
    face_ref[0:1, :] += side_ref[0:1, :] + corner_ref[...]
    slab_out = pltpu.make_async_copy(face_ref, out_ref.at[0], sem.at[2])
    slab_out.start()
    band.wait()
    for x in range(1, CX):
        band_ref[x - 1, 0:1, :] += side_ref[x:x + 1, :]
    band_out = pltpu.make_async_copy(band_ref, out_ref.at[pl.ds(1, CX - 1), pl.ds(0, 8), :], sem.at[3])
    band_out.start()
    slab_out.wait()
    band_out.wait()


def halo_add(core, front, side, corner):
    vmem = pl.BlockSpec(memory_space=pltpu.VMEM)
    hbm = pl.BlockSpec(memory_space=pltpu.HBM)
    return pl.pallas_call(
        halo_kernel,
        out_shape=jax.ShapeDtypeStruct((CX, CY, NZ), f32),
        in_specs=[hbm, vmem, vmem, vmem],
        out_specs=hbm,
        input_output_aliases={0: 0},
        scratch_shapes=[
            pltpu.VMEM((CY, NZ), f32),
            pltpu.VMEM((CX - 1, 8, NZ), f32),
            pltpu.SemaphoreType.DMA((4,)),
        ],
        compiler_params=pltpu.CompilerParams(vmem_limit_bytes=HALF_VMEM),
        cost_estimate=pl.CostEstimate(flops=1000000, bytes_accessed=1500000, transcendentals=0),
        name="halo_add",
    )(core, front, side, corner)


ROWS = NODES * SLOTS * 8
MB = 256


def arrival_rows(heads):
    count = heads.shape[0]
    line = iota((128, 128), 0)
    lane = iota((128, 128), 1)
    spread = jnp.where(line % 16 == (lane // 8) % 4 * 4 + lane % 4, 1.0, 0.0).astype(bf16)
    labels = (heads + 0.5).astype(i32)
    digits = jnp.concatenate([(labels >> 4).astype(f32), (labels & 15).astype(f32)], axis=0).astype(bf16)
    wide = jnp.dot(digits, spread, preferred_element_type=f32)
    wide = wide[0:count, :] * 16.0 + wide[count:2 * count, :]
    wide = jnp.where(iota((count, 128), 0) % 4 == iota((count, 128), 1) // 32, wide, 0.0)
    shift = 64 * ((iota((1, 128), 1) // 4) % 2)
    return [
        (jnp.sum(wide[4 * k:4 * k + 4, :], axis=0, keepdims=True) + 0.5).astype(i32) + shift
        for k in range(count // 4)
    ]


def one_hot(lines, target):
    one = jnp.ones(target.shape, bf16)
    zero = jnp.zeros(target.shape, bf16)
    return jnp.concatenate(
        [jnp.where(jnp.broadcast_to(line, target.shape).astype(jnp.int16) == target, one, zero) for line in lines],
        axis=1,
    )


def arrival_terms(got_ref, first, count):
    parts = [got_ref[s, :, 0:SLOTS * 1024].reshape(SLOTS * 8, 128) for s in range(first, first + count)]
    high, low = two_terms(jnp.concatenate(parts, axis=0))
    return jnp.concatenate([high.astype(bf16), low.astype(bf16)], axis=1)


def coarse_kernel(home_ref, got_ref, send_ref, head_ref, sums_ref, part_ref, sem):
    terms = arrival_terms(got_ref, 0, NODES)
    lines = []
    for k, row in enumerate(arrival_rows(got_ref[:, 0, SLOTS * 1024:LINE])):
        head_ref[k:k + 1, :] = row
        lines.append((row >> 10) * 512 + ((row >> 7) & 7) * 64 + (row & 63))
    for m in range(1024 // MB):
        target = (iota((MB, 128), 0) + m * MB).astype(jnp.int16)
        product = jnp.dot(one_hot(lines, target), terms, preferred_element_type=f32)
        sums_ref[m * MB:(m + 1) * MB, :] = product[:, 0:128] + product[:, 128:256]
    lane = iota((64, 128), 1)
    fold_row = iota((512, 128), 0)
    fold_lane = iota((512, 128), 1)
    fold = jnp.where((fold_row // 128) * 32 + (fold_row % 64) // 2 == fold_lane, 1.0, 0.0).astype(bf16)
    for far in (0, 1):
        pieces = []
        for q in range(4):
            spot = (4 * far + q) * 64
            odd = sums_ref[512 + spot:512 + spot + 64, :]
            before = jnp.concatenate([jnp.zeros((8, 128), f32), odd[0:56, :]], axis=0)
            both = sums_ref[spot:spot + 64, :] + jnp.where(lane < 64, odd, before)
            pieces.append(jnp.concatenate(two_terms(both), axis=0).astype(bf16))
        folded = jnp.dot(jnp.concatenate(pieces, axis=1), fold, preferred_element_type=f32)
        part_ref[far * 64:far * 64 + 64, :] = folded[0:64, :] + folded[64:128, :]
    copies = []
    for box in range(BPH):
        for far in (0, 1):
            hot = part_ref[pl.ds(far * 64 + box, 8, stride=8), :]
            part_ref[128 + box * 16 + far * 8:128 + box * 16 + far * 8 + 8, :] = hot
    for box in range(BPH):
        copy = pltpu.make_async_copy(
            part_ref.at[pl.ds(128 + box * 16, 16), :], send_ref.at[home_ref[box]], sem.at[box]
        )
        copy.start()
        copies.append(copy)
    for copy in copies:
        copy.wait()


def coarse_deposit(homes, arrived):
    hbm = pl.BlockSpec(memory_space=pltpu.HBM)
    return pl.pallas_call(
        coarse_kernel,
        out_shape=(jax.ShapeDtypeStruct((NODES, 16, 128), f32), jax.ShapeDtypeStruct((32, 128), i32)),
        in_specs=[pl.BlockSpec(memory_space=pltpu.SMEM), pl.BlockSpec(memory_space=pltpu.VMEM)],
        out_specs=(hbm, pl.BlockSpec(memory_space=pltpu.VMEM)),
        scratch_shapes=[
            pltpu.VMEM((1024, 128), f32),
            pltpu.VMEM((256, 128), f32),
            pltpu.SemaphoreType.DMA((BPH,)),
        ],
        compiler_params=pltpu.CompilerParams(vmem_limit_bytes=HALF_VMEM),
        cost_estimate=pl.CostEstimate(flops=1000, bytes_accessed=1000, transcendentals=0),
        name="coarse_deposit",
    )(homes, arrived)


def fine_kernel(head_ref, got_ref, fine_ref, terms_ref, sums_ref, hot_ref):
    terms_ref[...] = arrival_terms(got_ref, 0, NODES)

    def block(m, carry):
        target = (iota((MB, 128), 0) + m * MB).astype(jnp.int16)
        hot_ref[...] = one_hot([head_ref[k:k + 1, :] for k in range(ROWS // 128)], target)
        product = jnp.dot(hot_ref[...], terms_ref[...], preferred_element_type=f32)
        sums_ref[pl.ds(pl.multiple_of(m * MB, MB), MB), :] = product[:, 0:128] + product[:, 128:256]
        return carry

    lax.fori_loop(0, 2048 // MB, block, 0)
    lane = iota((8, 128), 1)
    for x in range(16):
        for y in range(8):
            spot = (x * 8 + y) * 8
            odd = sums_ref[1024 + spot:1024 + spot + 8, :]
            before = sums_ref[1024 + spot - 8:1024 + spot, :] if y else jnp.zeros((8, 128), f32)
            cross = pltpu.roll(jnp.where(lane < 64, odd, before), 64, 1)
            fine_ref[:, spot * 16:spot * 16 + 128] = sums_ref[spot:spot + 8, :] + cross


def fine_deposit(header, arrived):
    vmem = pl.BlockSpec(memory_space=pltpu.VMEM)
    return pl.pallas_call(
        fine_kernel,
        out_shape=jax.ShapeDtypeStruct((BPH, 16384), f32),
        in_specs=[vmem, vmem],
        out_specs=vmem,
        scratch_shapes=[
            pltpu.VMEM((ROWS, 256), bf16),
            pltpu.VMEM((2048, 128), f32),
            pltpu.VMEM((MB, ROWS), bf16),
        ],
        compiler_params=pltpu.CompilerParams(vmem_limit_bytes=HALF_VMEM),
        cost_estimate=pl.CostEstimate(flops=2 * 2048 * ROWS * 256, bytes_accessed=4000000, transcendentals=0),
        name="fine_deposit",
    )(header, arrived)


def lattice_kernel(owner_ref, place_ref, base_ref, got_ref, out_ref, held_ref, block_ref, got_sem, in_sem, out_sem):
    def spot_of(n, grid):
        place = place_ref[n]
        rows = pl.ds(pl.multiple_of(((place >> 5) & 7) * 8, 8), 8)
        lanes = pl.ds(pl.multiple_of(((place >> 2) & 7) * 128, 128), 128)
        return grid.at[:, rows, lanes]

    copies = []
    for n in range(BPH):
        copies.append(pltpu.make_async_copy(got_ref.at[owner_ref[n]], held_ref.at[n], got_sem.at[n]))
        copies.append(pltpu.make_async_copy(spot_of(n, base_ref), block_ref.at[n], in_sem.at[n]))
    for copy in copies:
        copy.start()
    firsts = []
    for n in range(BPH):
        first = jnp.int32(n)
        for k in reversed(range(n)):
            first = jnp.where(place_ref[k] >> 2 == place_ref[n] >> 2, k, first)
        firsts.append(first)
    for copy in copies:
        copy.wait()
    quarter = iota((8, 128), 1) // 32
    for n in range(BPH):
        spot = place_ref[n] & 3
        for x in range(CX):
            value = held_ref[n, (x // 4) * 8:(x // 4) * 8 + 8, :]
            moved = pltpu.roll(value, ((spot - x % 4 + 4) & 3) * 32, 1)
            block_ref[firsts[n], x] += jnp.where(quarter == spot, moved, 0.0)
    for n in range(BPH):
        @pl.when(firsts[n] == n)
        def _():
            pltpu.make_async_copy(block_ref.at[n], spot_of(n, out_ref), out_sem.at[n]).start()
    for n in range(BPH):
        @pl.when(firsts[n] == n)
        def _():
            pltpu.make_async_copy(block_ref.at[n], spot_of(n, out_ref), out_sem.at[n]).wait()


def lattice_add(owners, places, base, arrived):
    smem = pl.BlockSpec(memory_space=pltpu.SMEM)
    hbm = pl.BlockSpec(memory_space=pltpu.HBM)
    return pl.pallas_call(
        lattice_kernel,
        out_shape=jax.ShapeDtypeStruct((CX, CY, NZ), f32),
        in_specs=[smem, smem, hbm, hbm],
        out_specs=hbm,
        input_output_aliases={2: 0},
        scratch_shapes=[
            pltpu.VMEM((BPH, 16, 128), f32),
            pltpu.VMEM((BPH, CX, 8, 128), f32),
            pltpu.SemaphoreType.DMA((BPH,)),
            pltpu.SemaphoreType.DMA((BPH,)),
            pltpu.SemaphoreType.DMA((BPH,)),
        ],
        compiler_params=pltpu.CompilerParams(vmem_limit_bytes=ALL_VMEM),
        cost_estimate=pl.CostEstimate(flops=1000000, bytes_accessed=1000000, transcendentals=0),
        name="lattice_add",
    )(owners, places, base, arrived)


def shards(
    base_column,
    base_zbin,
    base_frac,
    base_weight,
    fine_column,
    fine_zbin,
    fine_frac,
    fine_weight,
    tile_box,
    box_home,
    box_anchor,
):
    myself = lax.axis_index(AXES).astype(i32)
    homes = lax.dynamic_slice_in_dim(box_home, myself * BPH, BPH, 0)
    outgoing = fine_profiles(tile_box, fine_column, fine_zbin, fine_frac, fine_weight)
    outgoing, base_column, myself = lax.optimization_barrier((outgoing, base_column, myself))
    arrived = lax.all_to_all(outgoing, AXES, split_axis=0, concat_axis=0, tiled=True)
    owners, places = tables(myself.reshape(1), box_home, box_anchor)
    core, front, side, corner = base_deposit(base_column, base_zbin, base_frac, base_weight)
    outer = (shifted(front, "blk", 1), shifted(side, "cross", 1), diagonal(corner))
    arrived, core, owners, places = lax.optimization_barrier((arrived, core, owners, places))
    sending, header = coarse_deposit(homes, arrived)
    sending, header, front, side, corner = lax.optimization_barrier((sending, header, *outer))
    returned = lax.all_to_all(sending, AXES, split_axis=0, concat_axis=0, tiled=True)
    fine_rows = fine_deposit(header, arrived)
    base = halo_add(core, front, side, corner)
    returned, base, fine_rows = lax.optimization_barrier((returned, base, fine_rows))
    base_out = lattice_add(owners, places, base, returned)
    return (base_out, fine_rows)


def solution(mesh):
    placed = (
        P(("blk", "cross")),
        P(("blk", "cross"), None),
        P(None, ("blk", "cross"), None),
        P(("blk", "cross"), None),
        P(("blk", "cross")),
        P(("blk", "cross"), None),
        P(None, ("blk", "cross"), None),
        P(("blk", "cross"), None),
        P(("blk", "cross")),
        P(),
        P(),
    )
    return jax.shard_map(
        shards,
        mesh=mesh,
        in_specs=placed,
        out_specs=(P("blk", "cross", None), P(("blk", "cross"), None)),
        check_vma=False,
    )
```

```python
import jax
import jax.numpy as jnp
from jax import lax
from jax.experimental import pallas as pl
from jax.experimental.pallas import tpu as pltpu
from jax.sharding import PartitionSpec as P

CX = 8
CY = 64
NZ = 1024
BPH = 8
NODES = 128
PT = 128
BT = 256
FT = 896
GROUPS = FT // 4
SLOTS = 4
GX = CX + 1
GY = CY + 1
AXES = ("blk", "cross")
PARTS = 4
ZL = 16
CHUNKS = 8
LINE = SLOTS * 1024 + 128
VMEM_BYTES = 62 * 1024 * 1024
ALL_VMEM = 63 * 1024 * 1024 + 512 * 1024
HALF_VMEM = 32 * 1024 * 1024
f32 = jnp.float32
bf16 = jnp.bfloat16
i32 = jnp.int32


def shifted(value, axis, steps):
    count = lax.axis_size(axis)
    pairs = [(source, (source + steps) % count) for source in range(count)]
    return lax.ppermute(value, axis, pairs)


def diagonal(value):
    blocks, columns = lax.axis_size("blk"), lax.axis_size("cross")
    pairs = [
        (b * columns + c, (b + 1) % blocks * columns + (c + 1) % columns)
        for b in range(blocks)
        for c in range(columns)
    ]
    return lax.ppermute(value, AXES, pairs)


def iota(shape, dim):
    return lax.broadcasted_iota(i32, shape, dim)


def two_terms(value):
    high = value.astype(bf16).astype(f32)
    return high, value - high


def nt_dot(left, right):
    return lax.dot_general(left, right, (((1,), (1,)), ((), ())), preferred_element_type=f32)


def corner_weights(u, v, w, m):
    result = []
    for part_x in (1.0 - u, u):
        row = []
        for part_y in (1.0 - v, v):
            plane = m * part_x * part_y
            row.append((plane * (1.0 - w), plane * w))
        result.append(row)
    return result


def fine_profile_kernel(
    box_ref, boxes_ref, columns_ref, zbin_ref, frac_ref, mass_ref, send_ref, out_ref, label_ref, head_ref, last_ref, sem
):
    part = pl.program_id(0)

    @pl.when(part == 0)
    def _():
        out_ref[...] = jnp.zeros(out_ref.shape, f32)
        boxes = boxes_ref[...]
        columns = columns_ref[...]
        x = (columns * 4370) >> 16
        y = columns - x * 15
        label_ref[...] = ((y & 1) * 1024 + (x * 8 + (y >> 1)) * 8 + (boxes & 7)).astype(f32)
        head_ref[...] = jnp.zeros((1, 128), f32)
        last_ref[0] = -1
        last_ref[1] = 0

    four_lanes = iota((1, 128), 1) // 4
    sub = iota((8, PT), 0)
    turn = (iota((8, PT), 1) // ZL + sub) & 7
    z_row = iota((ZL, PT), 0).astype(f32).astype(bf16)
    one = jnp.ones((ZL, PT), bf16)
    zero = jnp.zeros((ZL, PT), bf16)
    none = jnp.zeros((16, PT), bf16)
    uppers = 64 // ZL

    def step(i, carry):
        last, head = carry
        rows = pl.ds(pl.multiple_of(i * 8, 8), 8)
        z = zbin_ref[rows, :]
        weights = corner_weights(frac_ref[0, rows, :], frac_ref[1, rows, :], frac_ref[2, rows, :], mass_ref[rows, :])
        left = []
        right = []
        for e in (0, 1):
            cell = z + e
            upper = (cell // ZL).astype(f32)
            upper = jnp.concatenate([upper, upper], axis=0).astype(bf16)
            masks = [upper == none + h for h in range(uppers)]
            parts = []
            for a in (0, 1):
                for b in (0, 1):
                    terms = jnp.concatenate(two_terms(weights[a][b][e]), axis=0).astype(bf16)
                    for mask in masks:
                        parts.append(jnp.where(mask, terms, none))
            left.append(jnp.concatenate(parts, axis=0))
            lower = (cell & (ZL - 1)).astype(f32)
            hots = []
            for t in reversed(range(8)):
                row = jnp.broadcast_to(lower[t:t + 1, :], (ZL, PT)).astype(bf16)
                hots.append(jnp.where(row == z_row, one, zero))
            right.append(jnp.concatenate(hots, axis=0))
        product = nt_dot(jnp.concatenate(left, axis=1), jnp.concatenate(right, axis=1))
        halves = []
        for a in (0, 1):
            gathered = None
            for q in range(2 * uppers):
                start = (2 * uppers * a + q) * 16
                total = product[start:start + 8, :] + product[start + 8:start + 16, :]
                value = pltpu.roll(total, ZL * (q + 1), 1) if q < 7 else total
                gathered = value if gathered is None else jnp.where(turn == q, value, gathered)
            halves.append(pltpu.roll(gathered, 0, 1, stride=ZL, stride_axis=0))
        first = jnp.where(sub < 4, halves[0], pltpu.roll(halves[1], 4, 0))
        second = jnp.where(sub < 4, pltpu.roll(halves[0], 4, 0), halves[1])
        for g, value in ((0, first), (1, second)):
            group = part * (FT // PARTS // 4) + i * 2 + g
            owner = box_ref[group * 4] >> 3
            out_ref[owner, :, pl.ds(pl.multiple_of((group & 3) * 1024, 1024), 1024)] = value.reshape(1, 1024)
            label = jnp.where(four_lanes == (group & 31), label_ref[pl.ds(group >> 5, 1), :], 0.0)
            head = jnp.where(owner == last, head, 0.0) + label
            last = owner
            out_ref[owner, :, 4096:4224] = head
        return last, head

    steps = FT // PARTS // 8
    last, head = lax.fori_loop(0, steps, step, (last_ref[0], head_ref[...]), unroll=steps)
    last_ref[0] = last
    head_ref[...] = head
    span = NODES // CHUNKS
    copies = [
        pltpu.make_async_copy(out_ref.at[pl.ds(c * span, span)], send_ref.at[pl.ds(c * span, span)], sem.at[c])
        for c in range(CHUNKS)
    ]
    sent = last_ref[1]
    ready = jnp.where(part == PARTS - 1, CHUNKS, last // span)
    for c in range(CHUNKS):
        @pl.when((c >= sent) & (c < ready))
        def _():
            copies[c].start()
    last_ref[1] = ready

    @pl.when(part == PARTS - 1)
    def _():
        for copy in copies:
            copy.wait()


def fine_profiles(tile_box, fine_column, fine_zbin, fine_frac, fine_weight):
    tiles = FT // PARTS
    return pl.pallas_call(
        fine_profile_kernel,
        out_shape=jax.ShapeDtypeStruct((NODES, 1, LINE), f32),
        grid=(PARTS,),
        in_specs=[
            pl.BlockSpec(memory_space=pltpu.SMEM),
            pl.BlockSpec((FT // 128, 128), lambda i: (0, 0)),
            pl.BlockSpec((FT // 128, 128), lambda i: (0, 0)),
            pl.BlockSpec((tiles, PT), lambda i: (i, 0)),
            pl.BlockSpec((3, tiles, PT), lambda i: (0, i, 0)),
            pl.BlockSpec((tiles, PT), lambda i: (i, 0)),
        ],
        out_specs=pl.BlockSpec(memory_space=pltpu.HBM),
        scratch_shapes=[
            pltpu.VMEM((NODES, 1, LINE), f32),
            pltpu.VMEM((FT // 128, 128), f32),
            pltpu.VMEM((1, 128), f32),
            pltpu.SMEM((2,), i32),
            pltpu.SemaphoreType.DMA((CHUNKS,)),
        ],
        compiler_params=pltpu.CompilerParams(vmem_limit_bytes=VMEM_BYTES),
        cost_estimate=pl.CostEstimate(flops=2 * 128 * 256 * 256 * 112, bytes_accessed=4500000, transcendentals=0),
        name="fine_profiles",
    )(
        tile_box,
        tile_box.reshape(FT // 128, 128),
        fine_column.reshape(FT // 128, 128),
        fine_zbin,
        fine_frac,
        fine_weight,
    )


def tables_kernel(me_ref, home_ref, anchor_ref, owner_ref, place_ref):
    index = iota((8, 128), 0) * 128 + iota((8, 128), 1)
    left = jnp.where(home_ref[...] == me_ref[0], index, NODES * BPH)
    for n in range(BPH):
        box = jnp.minimum(jnp.min(left), NODES * BPH - 1)
        left = jnp.where(left == box, NODES * BPH, left)
        owner_ref[n] = box >> 3
        place_ref[n] = anchor_ref[box]


def tables(me, box_home, box_anchor):
    smem = pl.BlockSpec(memory_space=pltpu.SMEM)
    return pl.pallas_call(
        tables_kernel,
        out_shape=(jax.ShapeDtypeStruct((BPH,), i32), jax.ShapeDtypeStruct((BPH,), i32)),
        in_specs=[smem, pl.BlockSpec(memory_space=pltpu.VMEM), smem],
        out_specs=(smem, smem),
        cost_estimate=pl.CostEstimate(flops=4000000, bytes_accessed=40000, transcendentals=0),
        name="tables",
    )(me, box_home.reshape(8, 128), box_anchor)


def base_kernel(column_ref, zbin_ref, frac_ref, mass_ref, core_ref, front_ref, side_ref, corner_ref, grid_ref):
    grid_ref[...] = jnp.zeros(grid_ref.shape, f32)
    upper_row = iota((8, PT), 0)
    lower_row = iota((128, PT), 0)

    def step(i, carry):
        rows = pl.ds(pl.multiple_of(i * 8, 8), 8)
        z = zbin_ref[rows, :]
        weights = corner_weights(frac_ref[0, rows, :], frac_ref[1, rows, :], frac_ref[2, rows, :], mass_ref[rows, :])
        cells = (z, (z + 1) & (NZ - 1))
        uppers = [cell >> 7 for cell in cells]
        lowers = [cell & 127 for cell in cells]
        for t in range(8):
            left = []
            right = []
            for e in (0, 1):
                mask = jnp.broadcast_to(uppers[e][t:t + 1, :], (8, PT)) == upper_row
                parts = []
                for a in (0, 1):
                    for b in (0, 1):
                        row = jnp.broadcast_to(weights[a][b][e][t:t + 1, :], (8, PT))
                        parts.extend(two_terms(jnp.where(mask, row, 0.0)))
                left.append(jnp.concatenate(parts, axis=0).astype(bf16))
                low = jnp.broadcast_to(lowers[e][t:t + 1, :], (128, PT))
                right.append(jnp.where(low == lower_row, 1.0, 0.0).astype(bf16))
            product = nt_dot(jnp.concatenate(left, axis=1), jnp.concatenate(right, axis=1))
            q = column_ref[i * 8 + t]
            corner = (q // CY) * GY + q % CY
            for a in (0, 1):
                for b in (0, 1):
                    start = (2 * a + b) * 16
                    place = pl.ds(pl.multiple_of((corner + a * GY + b) * 8, 8), 8)
                    grid_ref[place, :] += product[start:start + 8, :] + product[start + 8:start + 16, :]
        return carry

    lax.fori_loop(0, BT // 8, step, 0, unroll=2)
    for x in range(GX):
        for band in range(CY // 8):
            for part in range(8):
                rows = grid_ref[pl.ds((x * GY + band * 8) * 8 + part, 8, stride=8), :]
                if x < CX:
                    core_ref[x, band * 8:band * 8 + 8, part * 128:part * 128 + 128] = rows
                else:
                    front_ref[band * 8:band * 8 + 8, part * 128:part * 128 + 128] = rows
    for part in range(8):
        lanes = slice(part * 128, part * 128 + 128)
        side_ref[:, lanes] = grid_ref[pl.ds(CY * 8 + part, 8, stride=GY * 8), :]
        corner_row = (CX * GY + CY) * 8 + part
        corner_ref[0:1, lanes] = grid_ref[corner_row:corner_row + 1, :]


def base_deposit(base_column, base_zbin, base_frac, base_weight):
    vmem = pl.BlockSpec(memory_space=pltpu.VMEM)
    return pl.pallas_call(
        base_kernel,
        out_shape=(
            jax.ShapeDtypeStruct((CX, CY, NZ), f32),
            jax.ShapeDtypeStruct((CY, NZ), f32),
            jax.ShapeDtypeStruct((CX, NZ), f32),
            jax.ShapeDtypeStruct((1, NZ), f32),
        ),
        in_specs=[pl.BlockSpec(memory_space=pltpu.SMEM), vmem, vmem, vmem],
        out_specs=(vmem, vmem, vmem, vmem),
        scratch_shapes=[pltpu.VMEM((GX * GY * 8, 128), f32)],
        compiler_params=pltpu.CompilerParams(vmem_limit_bytes=HALF_VMEM),
        cost_estimate=pl.CostEstimate(flops=10000000000, bytes_accessed=5000000, transcendentals=0),
        name="base_deposit",
    )(base_column, base_zbin, base_frac, base_weight)


def halo_kernel(core_ref, front_ref, side_ref, corner_ref, out_ref, face_ref, band_ref, sem):
    slab = pltpu.make_async_copy(core_ref.at[0], face_ref, sem.at[0])
    band = pltpu.make_async_copy(core_ref.at[pl.ds(1, CX - 1), pl.ds(0, 8), :], band_ref, sem.at[1])
    slab.start()
    band.start()
    slab.wait()
    face_ref[...] += front_ref[...]
    face_ref[0:1, :] += side_ref[0:1, :] + corner_ref[...]
    slab_out = pltpu.make_async_copy(face_ref, out_ref.at[0], sem.at[2])
    slab_out.start()
    band.wait()
    for x in range(1, CX):
        band_ref[x - 1, 0:1, :] += side_ref[x:x + 1, :]
    band_out = pltpu.make_async_copy(band_ref, out_ref.at[pl.ds(1, CX - 1), pl.ds(0, 8), :], sem.at[3])
    band_out.start()
    slab_out.wait()
    band_out.wait()


def halo_add(core, front, side, corner):
    vmem = pl.BlockSpec(memory_space=pltpu.VMEM)
    hbm = pl.BlockSpec(memory_space=pltpu.HBM)
    return pl.pallas_call(
        halo_kernel,
        out_shape=jax.ShapeDtypeStruct((CX, CY, NZ), f32),
        in_specs=[hbm, vmem, vmem, vmem],
        out_specs=hbm,
        input_output_aliases={0: 0},
        scratch_shapes=[
            pltpu.VMEM((CY, NZ), f32),
            pltpu.VMEM((CX - 1, 8, NZ), f32),
            pltpu.SemaphoreType.DMA((4,)),
        ],
        compiler_params=pltpu.CompilerParams(vmem_limit_bytes=HALF_VMEM),
        cost_estimate=pl.CostEstimate(flops=1000000, bytes_accessed=1500000, transcendentals=0),
        name="halo_add",
    )(core, front, side, corner)


ROWS = NODES * SLOTS * 8
MB = 256


def arrival_rows(heads):
    count = heads.shape[0]
    line = iota((128, 128), 0)
    lane = iota((128, 128), 1)
    spread = jnp.where(line % 16 == (lane // 8) % 4 * 4 + lane % 4, 1.0, 0.0).astype(bf16)
    labels = (heads + 0.5).astype(i32)
    digits = jnp.concatenate([(labels >> 4).astype(f32), (labels & 15).astype(f32)], axis=0).astype(bf16)
    wide = jnp.dot(digits, spread, preferred_element_type=f32)
    wide = wide[0:count, :] * 16.0 + wide[count:2 * count, :]
    wide = jnp.where(iota((count, 128), 0) % 4 == iota((count, 128), 1) // 32, wide, 0.0)
    shift = 64 * ((iota((1, 128), 1) // 4) % 2)
    return [
        (jnp.sum(wide[4 * k:4 * k + 4, :], axis=0, keepdims=True) + 0.5).astype(i32) + shift
        for k in range(count // 4)
    ]


def one_hot(lines, target):
    one = jnp.ones(target.shape, bf16)
    zero = jnp.zeros(target.shape, bf16)
    return jnp.concatenate(
        [jnp.where(jnp.broadcast_to(line, target.shape).astype(jnp.int16) == target, one, zero) for line in lines],
        axis=1,
    )


def arrival_terms(got_ref, first, count):
    parts = [got_ref[s, :, 0:SLOTS * 1024].reshape(SLOTS * 8, 128) for s in range(first, first + count)]
    high, low = two_terms(jnp.concatenate(parts, axis=0))
    return jnp.concatenate([high.astype(bf16), low.astype(bf16)], axis=1)


def coarse_kernel(home_ref, got_ref, send_ref, head_ref, sums_ref, part_ref, sem):
    heads = got_ref[:, 0, SLOTS * 1024:LINE]
    lines = []
    for k, row in enumerate(arrival_rows(heads)):
        head_ref[k:k + 1, :] = row
        lines.append(((row >> 7) & 7) * 64 + (row & 63))
    line = iota((32, 128), 0)
    spots = jnp.where(iota((32, 128), 1) % 16 == line // 8 * 4 + line % 4, 1.0, 0.0).astype(bf16)
    odd = nt_dot(spots, (((heads + 0.5).astype(i32) >> 10) & 1).astype(f32).astype(bf16))
    near = iota((32, 128), 1) < 64
    parts = []
    for s in range(NODES):
        value = got_ref[s, :, 0:SLOTS * 1024].reshape(SLOTS * 8, 128)
        level = jnp.where(near, value + pltpu.roll(value, 64, 1), 0.0)
        parts.append(jnp.where(jnp.broadcast_to(odd[:, s:s + 1], (32, 128)) > 0.5, value, level))
    high, low = two_terms(jnp.concatenate(parts, axis=0))
    terms = jnp.concatenate([high.astype(bf16), low.astype(bf16)], axis=1)
    for m in range(512 // MB):
        target = (iota((MB, 128), 0) + m * MB).astype(jnp.int16)
        product = jnp.dot(one_hot(lines, target), terms, preferred_element_type=f32)
        sums_ref[m * MB:(m + 1) * MB, :] = product[:, 0:128] + product[:, 128:256]
    lane = iota((64, 128), 1)
    fold_row = iota((512, 128), 0)
    fold_lane = iota((512, 128), 1)
    fold = jnp.where((fold_row // 128) * 32 + (fold_row % 64) // 2 == fold_lane, 1.0, 0.0).astype(bf16)
    for far in (0, 1):
        pieces = []
        for q in range(4):
            spot = (4 * far + q) * 64
            here = sums_ref[spot:spot + 64, :]
            before = jnp.concatenate([jnp.zeros((8, 128), f32), here[0:56, :]], axis=0)
            both = jnp.where(lane < 64, here, before)
            pieces.append(jnp.concatenate(two_terms(both), axis=0).astype(bf16))
        folded = jnp.dot(jnp.concatenate(pieces, axis=1), fold, preferred_element_type=f32)
        part_ref[far * 64:far * 64 + 64, :] = folded[0:64, :] + folded[64:128, :]
    copies = []
    for box in range(BPH):
        for far in (0, 1):
            hot = part_ref[pl.ds(far * 64 + box, 8, stride=8), :]
            part_ref[128 + box * 16 + far * 8:128 + box * 16 + far * 8 + 8, :] = hot
    for box in range(BPH):
        copy = pltpu.make_async_copy(
            part_ref.at[pl.ds(128 + box * 16, 16), :], send_ref.at[home_ref[box]], sem.at[box]
        )
        copy.start()
        copies.append(copy)
    for copy in copies:
        copy.wait()


def coarse_deposit(homes, arrived):
    hbm = pl.BlockSpec(memory_space=pltpu.HBM)
    return pl.pallas_call(
        coarse_kernel,
        out_shape=(jax.ShapeDtypeStruct((NODES, 16, 128), f32), jax.ShapeDtypeStruct((32, 128), i32)),
        in_specs=[pl.BlockSpec(memory_space=pltpu.SMEM), pl.BlockSpec(memory_space=pltpu.VMEM)],
        out_specs=(hbm, pl.BlockSpec(memory_space=pltpu.VMEM)),
        scratch_shapes=[
            pltpu.VMEM((512, 128), f32),
            pltpu.VMEM((256, 128), f32),
            pltpu.SemaphoreType.DMA((BPH,)),
        ],
        compiler_params=pltpu.CompilerParams(vmem_limit_bytes=HALF_VMEM),
        cost_estimate=pl.CostEstimate(flops=1000, bytes_accessed=1000, transcendentals=0),
        name="coarse_deposit",
    )(homes, arrived)


def fine_kernel(head_ref, got_ref, fine_ref, terms_ref, sums_ref, hot_ref):
    terms_ref[...] = arrival_terms(got_ref, 0, NODES)

    def block(m, carry):
        target = (iota((MB, 128), 0) + m * MB).astype(jnp.int16)
        hot_ref[...] = one_hot([head_ref[k:k + 1, :] for k in range(ROWS // 128)], target)
        product = jnp.dot(hot_ref[...], terms_ref[...], preferred_element_type=f32)
        sums_ref[pl.ds(pl.multiple_of(m * MB, MB), MB), :] = product[:, 0:128] + product[:, 128:256]
        return carry

    lax.fori_loop(0, 2048 // MB, block, 0)
    lane = iota((8, 128), 1)
    for x in range(16):
        for y in range(8):
            spot = (x * 8 + y) * 8
            odd = sums_ref[1024 + spot:1024 + spot + 8, :]
            before = sums_ref[1024 + spot - 8:1024 + spot, :] if y else jnp.zeros((8, 128), f32)
            cross = pltpu.roll(jnp.where(lane < 64, odd, before), 64, 1)
            fine_ref[:, spot * 16:spot * 16 + 128] = sums_ref[spot:spot + 8, :] + cross


def fine_deposit(header, arrived):
    vmem = pl.BlockSpec(memory_space=pltpu.VMEM)
    return pl.pallas_call(
        fine_kernel,
        out_shape=jax.ShapeDtypeStruct((BPH, 16384), f32),
        in_specs=[vmem, vmem],
        out_specs=vmem,
        scratch_shapes=[
            pltpu.VMEM((ROWS, 256), bf16),
            pltpu.VMEM((2048, 128), f32),
            pltpu.VMEM((MB, ROWS), bf16),
        ],
        compiler_params=pltpu.CompilerParams(vmem_limit_bytes=HALF_VMEM),
        cost_estimate=pl.CostEstimate(flops=2 * 2048 * ROWS * 256, bytes_accessed=4000000, transcendentals=0),
        name="fine_deposit",
    )(header, arrived)


def lattice_kernel(owner_ref, place_ref, base_ref, got_ref, out_ref, held_ref, block_ref, got_sem, in_sem, out_sem):
    def spot_of(n, grid):
        place = place_ref[n]
        rows = pl.ds(pl.multiple_of(((place >> 5) & 7) * 8, 8), 8)
        lanes = pl.ds(pl.multiple_of(((place >> 2) & 7) * 128, 128), 128)
        return grid.at[:, rows, lanes]

    copies = []
    for n in range(BPH):
        copies.append(pltpu.make_async_copy(got_ref.at[owner_ref[n]], held_ref.at[n], got_sem.at[n]))
        copies.append(pltpu.make_async_copy(spot_of(n, base_ref), block_ref.at[n], in_sem.at[n]))
    for copy in copies:
        copy.start()
    firsts = []
    for n in range(BPH):
        first = jnp.int32(n)
        for k in reversed(range(n)):
            first = jnp.where(place_ref[k] >> 2 == place_ref[n] >> 2, k, first)
        firsts.append(first)
    for copy in copies:
        copy.wait()
    quarter = iota((8, 128), 1) // 32
    for n in range(BPH):
        spot = place_ref[n] & 3
        for x in range(CX):
            value = held_ref[n, (x // 4) * 8:(x // 4) * 8 + 8, :]
            moved = pltpu.roll(value, ((spot - x % 4 + 4) & 3) * 32, 1)
            block_ref[firsts[n], x] += jnp.where(quarter == spot, moved, 0.0)
    for n in range(BPH):
        @pl.when(firsts[n] == n)
        def _():
            pltpu.make_async_copy(block_ref.at[n], spot_of(n, out_ref), out_sem.at[n]).start()
    for n in range(BPH):
        @pl.when(firsts[n] == n)
        def _():
            pltpu.make_async_copy(block_ref.at[n], spot_of(n, out_ref), out_sem.at[n]).wait()


def lattice_add(owners, places, base, arrived):
    smem = pl.BlockSpec(memory_space=pltpu.SMEM)
    hbm = pl.BlockSpec(memory_space=pltpu.HBM)
    return pl.pallas_call(
        lattice_kernel,
        out_shape=jax.ShapeDtypeStruct((CX, CY, NZ), f32),
        in_specs=[smem, smem, hbm, hbm],
        out_specs=hbm,
        input_output_aliases={2: 0},
        scratch_shapes=[
            pltpu.VMEM((BPH, 16, 128), f32),
            pltpu.VMEM((BPH, CX, 8, 128), f32),
            pltpu.SemaphoreType.DMA((BPH,)),
            pltpu.SemaphoreType.DMA((BPH,)),
            pltpu.SemaphoreType.DMA((BPH,)),
        ],
        compiler_params=pltpu.CompilerParams(vmem_limit_bytes=ALL_VMEM),
        cost_estimate=pl.CostEstimate(flops=1000000, bytes_accessed=1000000, transcendentals=0),
        name="lattice_add",
    )(owners, places, base, arrived)


def shards(
    base_column,
    base_zbin,
    base_frac,
    base_weight,
    fine_column,
    fine_zbin,
    fine_frac,
    fine_weight,
    tile_box,
    box_home,
    box_anchor,
):
    myself = lax.axis_index(AXES).astype(i32)
    homes = lax.dynamic_slice_in_dim(box_home, myself * BPH, BPH, 0)
    outgoing = fine_profiles(tile_box, fine_column, fine_zbin, fine_frac, fine_weight)
    outgoing, base_column, myself = lax.optimization_barrier((outgoing, base_column, myself))
    arrived = lax.all_to_all(outgoing, AXES, split_axis=0, concat_axis=0, tiled=True)
    owners, places = tables(myself.reshape(1), box_home, box_anchor)
    core, front, side, corner = base_deposit(base_column, base_zbin, base_frac, base_weight)
    outer = (shifted(front, "blk", 1), shifted(side, "cross", 1), diagonal(corner))
    arrived, core, owners, places = lax.optimization_barrier((arrived, core, owners, places))
    sending, header = coarse_deposit(homes, arrived)
    sending, header, front, side, corner = lax.optimization_barrier((sending, header, *outer))
    returned = lax.all_to_all(sending, AXES, split_axis=0, concat_axis=0, tiled=True)
    fine_rows = fine_deposit(header, arrived)
    base = halo_add(core, front, side, corner)
    returned, base, fine_rows = lax.optimization_barrier((returned, base, fine_rows))
    base_out = lattice_add(owners, places, base, returned)
    return (base_out, fine_rows)


def solution(mesh):
    placed = (
        P(("blk", "cross")),
        P(("blk", "cross"), None),
        P(None, ("blk", "cross"), None),
        P(("blk", "cross"), None),
        P(("blk", "cross")),
        P(("blk", "cross"), None),
        P(None, ("blk", "cross"), None),
        P(("blk", "cross"), None),
        P(("blk", "cross")),
        P(),
        P(),
    )
    return jax.shard_map(
        shards,
        mesh=mesh,
        in_specs=placed,
        out_specs=(P("blk", "cross", None), P(("blk", "cross"), None)),
        check_vma=False,
    )
```

```python
import jax
import jax.numpy as jnp
from jax import lax
from jax.experimental import pallas as pl
from jax.experimental.pallas import tpu as pltpu
from jax.sharding import PartitionSpec as P

CX = 8
CY = 64
NZ = 1024
BPH = 8
NODES = 128
PT = 128
BT = 256
FT = 896
GROUPS = FT // 4
SLOTS = 4
GX = CX + 1
GY = CY + 1
AXES = ("blk", "cross")
PARTS = 4
ZL = 16
CHUNKS = 8
LINE = SLOTS * 1024 + 128
VMEM_BYTES = 62 * 1024 * 1024
ALL_VMEM = 63 * 1024 * 1024 + 512 * 1024
HALF_VMEM = 32 * 1024 * 1024
f32 = jnp.float32
bf16 = jnp.bfloat16
i32 = jnp.int32


def shifted(value, axis, steps):
    count = lax.axis_size(axis)
    pairs = [(source, (source + steps) % count) for source in range(count)]
    return lax.ppermute(value, axis, pairs)


def diagonal(value):
    blocks, columns = lax.axis_size("blk"), lax.axis_size("cross")
    pairs = [
        (b * columns + c, (b + 1) % blocks * columns + (c + 1) % columns)
        for b in range(blocks)
        for c in range(columns)
    ]
    return lax.ppermute(value, AXES, pairs)


def iota(shape, dim):
    return lax.broadcasted_iota(i32, shape, dim)


def two_terms(value):
    high = value.astype(bf16).astype(f32)
    return high, value - high


def nt_dot(left, right):
    return lax.dot_general(left, right, (((1,), (1,)), ((), ())), preferred_element_type=f32)


def corner_weights(u, v, w, m):
    result = []
    for part_x in (1.0 - u, u):
        row = []
        for part_y in (1.0 - v, v):
            plane = m * part_x * part_y
            row.append((plane * (1.0 - w), plane * w))
        result.append(row)
    return result


def fine_profile_kernel(
    box_ref, boxes_ref, columns_ref, zbin_ref, frac_ref, mass_ref, send_ref, out_ref, label_ref, head_ref, last_ref, sem
):
    part = pl.program_id(0)

    @pl.when(part == 0)
    def _():
        out_ref[...] = jnp.zeros(out_ref.shape, f32)
        boxes = boxes_ref[...]
        columns = columns_ref[...]
        x = (columns * 4370) >> 16
        y = columns - x * 15
        label_ref[...] = ((y & 1) * 1024 + (x * 8 + (y >> 1)) * 8 + (boxes & 7)).astype(f32)
        head_ref[...] = jnp.zeros((1, 128), f32)
        last_ref[0] = -1
        last_ref[1] = 0

    four_lanes = iota((1, 128), 1) // 4
    sub = iota((8, PT), 0)
    turn = (iota((8, PT), 1) // ZL + sub) & 7
    z_row = iota((ZL, PT), 0).astype(f32).astype(bf16)
    one = jnp.ones((ZL, PT), bf16)
    zero = jnp.zeros((ZL, PT), bf16)
    none = jnp.zeros((16, PT), bf16)
    uppers = 64 // ZL

    def step(i, carry):
        last, head = carry
        rows = pl.ds(pl.multiple_of(i * 8, 8), 8)
        z = zbin_ref[rows, :]
        weights = corner_weights(frac_ref[0, rows, :], frac_ref[1, rows, :], frac_ref[2, rows, :], mass_ref[rows, :])
        left = []
        right = []
        for e in (0, 1):
            cell = z + e
            upper = (cell // ZL).astype(f32)
            upper = jnp.concatenate([upper, upper], axis=0).astype(bf16)
            masks = [upper == none + h for h in range(uppers)]
            parts = []
            for a in (0, 1):
                for b in (0, 1):
                    terms = jnp.concatenate(two_terms(weights[a][b][e]), axis=0).astype(bf16)
                    for mask in masks:
                        parts.append(jnp.where(mask, terms, none))
            left.append(jnp.concatenate(parts, axis=0))
            lower = (cell & (ZL - 1)).astype(f32)
            hots = []
            for t in reversed(range(8)):
                row = jnp.broadcast_to(lower[t:t + 1, :], (ZL, PT)).astype(bf16)
                hots.append(jnp.where(row == z_row, one, zero))
            right.append(jnp.concatenate(hots, axis=0))
        product = nt_dot(jnp.concatenate(left, axis=1), jnp.concatenate(right, axis=1))
        halves = []
        for a in (0, 1):
            gathered = None
            for q in range(2 * uppers):
                start = (2 * uppers * a + q) * 16
                total = product[start:start + 8, :] + product[start + 8:start + 16, :]
                value = pltpu.roll(total, ZL * (q + 1), 1) if q < 7 else total
                gathered = value if gathered is None else jnp.where(turn == q, value, gathered)
            halves.append(pltpu.roll(gathered, 0, 1, stride=ZL, stride_axis=0))
        first = jnp.where(sub < 4, halves[0], pltpu.roll(halves[1], 4, 0))
        second = jnp.where(sub < 4, pltpu.roll(halves[0], 4, 0), halves[1])
        for g, value in ((0, first), (1, second)):
            group = part * (FT // PARTS // 4) + i * 2 + g
            owner = box_ref[group * 4] >> 3
            out_ref[owner, :, pl.ds(pl.multiple_of((group & 3) * 1024, 1024), 1024)] = value.reshape(1, 1024)
            label = jnp.where(four_lanes == (group & 31), label_ref[pl.ds(group >> 5, 1), :], 0.0)
            head = jnp.where(owner == last, head, 0.0) + label
            last = owner
            out_ref[owner, :, 4096:4224] = head
        return last, head

    steps = FT // PARTS // 8
    last, head = lax.fori_loop(0, steps, step, (last_ref[0], head_ref[...]), unroll=steps)
    last_ref[0] = last
    head_ref[...] = head
    span = NODES // CHUNKS
    copies = [
        pltpu.make_async_copy(out_ref.at[pl.ds(c * span, span)], send_ref.at[pl.ds(c * span, span)], sem.at[c])
        for c in range(CHUNKS)
    ]
    sent = last_ref[1]
    ready = jnp.where(part == PARTS - 1, CHUNKS, last // span)
    for c in range(CHUNKS):
        @pl.when((c >= sent) & (c < ready))
        def _():
            copies[c].start()
    last_ref[1] = ready

    @pl.when(part == PARTS - 1)
    def _():
        for copy in copies:
            copy.wait()


def fine_profiles(tile_box, fine_column, fine_zbin, fine_frac, fine_weight):
    tiles = FT // PARTS
    return pl.pallas_call(
        fine_profile_kernel,
        out_shape=jax.ShapeDtypeStruct((NODES, 1, LINE), f32),
        grid=(PARTS,),
        in_specs=[
            pl.BlockSpec(memory_space=pltpu.SMEM),
            pl.BlockSpec((FT // 128, 128), lambda i: (0, 0)),
            pl.BlockSpec((FT // 128, 128), lambda i: (0, 0)),
            pl.BlockSpec((tiles, PT), lambda i: (i, 0)),
            pl.BlockSpec((3, tiles, PT), lambda i: (0, i, 0)),
            pl.BlockSpec((tiles, PT), lambda i: (i, 0)),
        ],
        out_specs=pl.BlockSpec(memory_space=pltpu.HBM),
        scratch_shapes=[
            pltpu.VMEM((NODES, 1, LINE), f32),
            pltpu.VMEM((FT // 128, 128), f32),
            pltpu.VMEM((1, 128), f32),
            pltpu.SMEM((2,), i32),
            pltpu.SemaphoreType.DMA((CHUNKS,)),
        ],
        compiler_params=pltpu.CompilerParams(vmem_limit_bytes=VMEM_BYTES),
        cost_estimate=pl.CostEstimate(flops=2 * 128 * 256 * 256 * 112, bytes_accessed=4500000, transcendentals=0),
        name="fine_profiles",
    )(
        tile_box,
        tile_box.reshape(FT // 128, 128),
        fine_column.reshape(FT // 128, 128),
        fine_zbin,
        fine_frac,
        fine_weight,
    )


def tables_kernel(me_ref, home_ref, anchor_ref, owner_ref, place_ref):
    index = iota((8, 128), 0) * 128 + iota((8, 128), 1)
    left = jnp.where(home_ref[...] == me_ref[0], index, NODES * BPH)
    for n in range(BPH):
        box = jnp.minimum(jnp.min(left), NODES * BPH - 1)
        left = jnp.where(left == box, NODES * BPH, left)
        owner_ref[n] = box >> 3
        place_ref[n] = anchor_ref[box]


def tables(me, box_home, box_anchor):
    smem = pl.BlockSpec(memory_space=pltpu.SMEM)
    return pl.pallas_call(
        tables_kernel,
        out_shape=(jax.ShapeDtypeStruct((BPH,), i32), jax.ShapeDtypeStruct((BPH,), i32)),
        in_specs=[smem, pl.BlockSpec(memory_space=pltpu.VMEM), smem],
        out_specs=(smem, smem),
        cost_estimate=pl.CostEstimate(flops=4000000, bytes_accessed=40000, transcendentals=0),
        name="tables",
    )(me, box_home.reshape(8, 128), box_anchor)


def base_kernel(column_ref, zbin_ref, frac_ref, mass_ref, core_ref, front_ref, side_ref, corner_ref, grid_ref):
    grid_ref[...] = jnp.zeros(grid_ref.shape, f32)
    upper_row = iota((8, PT), 0)
    lower_row = iota((128, PT), 0)

    def step(i, carry):
        rows = pl.ds(pl.multiple_of(i * 8, 8), 8)
        z = zbin_ref[rows, :]
        weights = corner_weights(frac_ref[0, rows, :], frac_ref[1, rows, :], frac_ref[2, rows, :], mass_ref[rows, :])
        cells = (z, (z + 1) & (NZ - 1))
        uppers = [cell >> 7 for cell in cells]
        lowers = [cell & 127 for cell in cells]
        for t in range(8):
            left = []
            right = []
            for e in (0, 1):
                mask = jnp.broadcast_to(uppers[e][t:t + 1, :], (8, PT)) == upper_row
                parts = []
                for a in (0, 1):
                    for b in (0, 1):
                        row = jnp.broadcast_to(weights[a][b][e][t:t + 1, :], (8, PT))
                        parts.extend(two_terms(jnp.where(mask, row, 0.0)))
                left.append(jnp.concatenate(parts, axis=0).astype(bf16))
                low = jnp.broadcast_to(lowers[e][t:t + 1, :], (128, PT))
                right.append(jnp.where(low == lower_row, 1.0, 0.0).astype(bf16))
            product = nt_dot(jnp.concatenate(left, axis=1), jnp.concatenate(right, axis=1))
            q = column_ref[i * 8 + t]
            corner = (q // CY) * GY + q % CY
            for a in (0, 1):
                for b in (0, 1):
                    start = (2 * a + b) * 16
                    place = pl.ds(pl.multiple_of((corner + a * GY + b) * 8, 8), 8)
                    grid_ref[place, :] += product[start:start + 8, :] + product[start + 8:start + 16, :]
        return carry

    lax.fori_loop(0, BT // 8, step, 0, unroll=2)
    for x in range(GX):
        for band in range(CY // 8):
            for part in range(8):
                rows = grid_ref[pl.ds((x * GY + band * 8) * 8 + part, 8, stride=8), :]
                if x < CX:
                    core_ref[x, band * 8:band * 8 + 8, part * 128:part * 128 + 128] = rows
                else:
                    front_ref[band * 8:band * 8 + 8, part * 128:part * 128 + 128] = rows
    for part in range(8):
        lanes = slice(part * 128, part * 128 + 128)
        side_ref[:, lanes] = grid_ref[pl.ds(CY * 8 + part, 8, stride=GY * 8), :]
        corner_row = (CX * GY + CY) * 8 + part
        corner_ref[0:1, lanes] = grid_ref[corner_row:corner_row + 1, :]


def base_deposit(base_column, base_zbin, base_frac, base_weight):
    vmem = pl.BlockSpec(memory_space=pltpu.VMEM)
    return pl.pallas_call(
        base_kernel,
        out_shape=(
            jax.ShapeDtypeStruct((CX, CY, NZ), f32),
            jax.ShapeDtypeStruct((CY, NZ), f32),
            jax.ShapeDtypeStruct((CX, NZ), f32),
            jax.ShapeDtypeStruct((1, NZ), f32),
        ),
        in_specs=[pl.BlockSpec(memory_space=pltpu.SMEM), vmem, vmem, vmem],
        out_specs=(vmem, vmem, vmem, vmem),
        scratch_shapes=[pltpu.VMEM((GX * GY * 8, 128), f32)],
        compiler_params=pltpu.CompilerParams(vmem_limit_bytes=HALF_VMEM),
        cost_estimate=pl.CostEstimate(flops=10000000000, bytes_accessed=5000000, transcendentals=0),
        name="base_deposit",
    )(base_column, base_zbin, base_frac, base_weight)


def box_spot(place, grid):
    rows = pl.ds(pl.multiple_of(((place >> 5) & 7) * 8, 8), 8)
    lanes = pl.ds(pl.multiple_of(((place >> 2) & 7) * 128, 128), 128)
    return grid.at[:, rows, lanes]


def halo_kernel(
    place_ref, core_ref, front_ref, side_ref, corner_ref, out_ref, block_ref, face_ref, band_ref, sem, block_sem
):
    slab = pltpu.make_async_copy(core_ref.at[0], face_ref, sem.at[0])
    band = pltpu.make_async_copy(core_ref.at[pl.ds(1, CX - 1), pl.ds(0, 8), :], band_ref, sem.at[1])
    slab.start()
    band.start()
    slab.wait()
    face_ref[...] += front_ref[...]
    face_ref[0:1, :] += side_ref[0:1, :] + corner_ref[...]
    slab_out = pltpu.make_async_copy(face_ref, out_ref.at[0], sem.at[2])
    slab_out.start()
    band.wait()
    for x in range(1, CX):
        band_ref[x - 1, 0:1, :] += side_ref[x:x + 1, :]
    band_out = pltpu.make_async_copy(band_ref, out_ref.at[pl.ds(1, CX - 1), pl.ds(0, 8), :], sem.at[3])
    band_out.start()
    slab_out.wait()
    band_out.wait()
    copies = [
        pltpu.make_async_copy(box_spot(place_ref[n], out_ref), block_ref.at[n], block_sem.at[n]) for n in range(BPH)
    ]
    for copy in copies:
        copy.start()
    for copy in copies:
        copy.wait()


def halo_add(places, core, front, side, corner):
    vmem = pl.BlockSpec(memory_space=pltpu.VMEM)
    hbm = pl.BlockSpec(memory_space=pltpu.HBM)
    return pl.pallas_call(
        halo_kernel,
        out_shape=(
            jax.ShapeDtypeStruct((CX, CY, NZ), f32),
            jax.ShapeDtypeStruct((BPH, CX, 8, 128), f32),
        ),
        in_specs=[pl.BlockSpec(memory_space=pltpu.SMEM), hbm, vmem, vmem, vmem],
        out_specs=(hbm, hbm),
        input_output_aliases={1: 0},
        scratch_shapes=[
            pltpu.VMEM((CY, NZ), f32),
            pltpu.VMEM((CX - 1, 8, NZ), f32),
            pltpu.SemaphoreType.DMA((4,)),
            pltpu.SemaphoreType.DMA((BPH,)),
        ],
        compiler_params=pltpu.CompilerParams(vmem_limit_bytes=HALF_VMEM),
        cost_estimate=pl.CostEstimate(flops=1000000, bytes_accessed=1500000, transcendentals=0),
        name="halo_add",
    )(places, core, front, side, corner)


ROWS = NODES * SLOTS * 8
MB = 256


def arrival_rows(heads):
    count = heads.shape[0]
    line = iota((128, 128), 0)
    lane = iota((128, 128), 1)
    spread = jnp.where(line % 16 == (lane // 8) % 4 * 4 + lane % 4, 1.0, 0.0).astype(bf16)
    labels = (heads + 0.5).astype(i32)
    digits = jnp.concatenate([(labels >> 4).astype(f32), (labels & 15).astype(f32)], axis=0).astype(bf16)
    wide = jnp.dot(digits, spread, preferred_element_type=f32)
    wide = wide[0:count, :] * 16.0 + wide[count:2 * count, :]
    wide = jnp.where(iota((count, 128), 0) % 4 == iota((count, 128), 1) // 32, wide, 0.0)
    shift = 64 * ((iota((1, 128), 1) // 4) % 2)
    return [
        (jnp.sum(wide[4 * k:4 * k + 4, :], axis=0, keepdims=True) + 0.5).astype(i32) + shift
        for k in range(count // 4)
    ]


def one_hot(lines, target):
    one = jnp.ones(target.shape, bf16)
    zero = jnp.zeros(target.shape, bf16)
    return jnp.concatenate(
        [jnp.where(jnp.broadcast_to(line, target.shape).astype(jnp.int16) == target, one, zero) for line in lines],
        axis=1,
    )


def arrival_terms(got_ref, first, count):
    parts = [got_ref[s, :, 0:SLOTS * 1024].reshape(SLOTS * 8, 128) for s in range(first, first + count)]
    high, low = two_terms(jnp.concatenate(parts, axis=0))
    return jnp.concatenate([high.astype(bf16), low.astype(bf16)], axis=1)


def coarse_kernel(home_ref, got_ref, send_ref, head_ref, sums_ref, part_ref, sem):
    heads = got_ref[:, 0, SLOTS * 1024:LINE]
    lines = []
    for k, row in enumerate(arrival_rows(heads)):
        head_ref[k:k + 1, :] = row
        lines.append(((row >> 7) & 7) * 64 + (row & 63))
    line = iota((32, 128), 0)
    spots = jnp.where(iota((32, 128), 1) % 16 == line // 8 * 4 + line % 4, 1.0, 0.0).astype(bf16)
    odd = nt_dot(spots, (((heads + 0.5).astype(i32) >> 10) & 1).astype(f32).astype(bf16))
    near = iota((32, 128), 1) < 64
    parts = []
    for s in range(NODES):
        value = got_ref[s, :, 0:SLOTS * 1024].reshape(SLOTS * 8, 128)
        level = jnp.where(near, value + pltpu.roll(value, 64, 1), 0.0)
        parts.append(jnp.where(jnp.broadcast_to(odd[:, s:s + 1], (32, 128)) > 0.5, value, level))
    high, low = two_terms(jnp.concatenate(parts, axis=0))
    terms = jnp.concatenate([high.astype(bf16), low.astype(bf16)], axis=1)
    for m in range(512 // MB):
        target = (iota((MB, 128), 0) + m * MB).astype(jnp.int16)
        product = jnp.dot(one_hot(lines, target), terms, preferred_element_type=f32)
        sums_ref[m * MB:(m + 1) * MB, :] = product[:, 0:128] + product[:, 128:256]
    lane = iota((64, 128), 1)
    fold_row = iota((512, 128), 0)
    fold_lane = iota((512, 128), 1)
    fold = jnp.where((fold_row // 128) * 32 + (fold_row % 64) // 2 == fold_lane, 1.0, 0.0).astype(bf16)
    for far in (0, 1):
        pieces = []
        for q in range(4):
            spot = (4 * far + q) * 64
            here = sums_ref[spot:spot + 64, :]
            before = jnp.concatenate([jnp.zeros((8, 128), f32), here[0:56, :]], axis=0)
            both = jnp.where(lane < 64, here, before)
            pieces.append(jnp.concatenate(two_terms(both), axis=0).astype(bf16))
        folded = jnp.dot(jnp.concatenate(pieces, axis=1), fold, preferred_element_type=f32)
        part_ref[far * 64:far * 64 + 64, :] = folded[0:64, :] + folded[64:128, :]
    copies = []
    for box in range(BPH):
        for far in (0, 1):
            hot = part_ref[pl.ds(far * 64 + box, 8, stride=8), :]
            part_ref[128 + box * 16 + far * 8:128 + box * 16 + far * 8 + 8, :] = hot
    for box in range(BPH):
        copy = pltpu.make_async_copy(
            part_ref.at[pl.ds(128 + box * 16, 16), :], send_ref.at[home_ref[box]], sem.at[box]
        )
        copy.start()
        copies.append(copy)
    for copy in copies:
        copy.wait()


def coarse_deposit(homes, arrived):
    hbm = pl.BlockSpec(memory_space=pltpu.HBM)
    return pl.pallas_call(
        coarse_kernel,
        out_shape=(jax.ShapeDtypeStruct((NODES, 16, 128), f32), jax.ShapeDtypeStruct((32, 128), i32)),
        in_specs=[pl.BlockSpec(memory_space=pltpu.SMEM), pl.BlockSpec(memory_space=pltpu.VMEM)],
        out_specs=(hbm, pl.BlockSpec(memory_space=pltpu.VMEM)),
        scratch_shapes=[
            pltpu.VMEM((512, 128), f32),
            pltpu.VMEM((256, 128), f32),
            pltpu.SemaphoreType.DMA((BPH,)),
        ],
        compiler_params=pltpu.CompilerParams(vmem_limit_bytes=HALF_VMEM),
        cost_estimate=pl.CostEstimate(flops=1000, bytes_accessed=1000, transcendentals=0),
        name="coarse_deposit",
    )(homes, arrived)


def fine_kernel(head_ref, got_ref, fine_ref, terms_ref, sums_ref, hot_ref):
    terms_ref[...] = arrival_terms(got_ref, 0, NODES)

    def block(m, carry):
        target = (iota((MB, 128), 0) + m * MB).astype(jnp.int16)
        hot_ref[...] = one_hot([head_ref[k:k + 1, :] for k in range(ROWS // 128)], target)
        product = jnp.dot(hot_ref[...], terms_ref[...], preferred_element_type=f32)
        sums_ref[pl.ds(pl.multiple_of(m * MB, MB), MB), :] = product[:, 0:128] + product[:, 128:256]
        return carry

    lax.fori_loop(0, 2048 // MB, block, 0)
    lane = iota((8, 128), 1)
    for x in range(16):
        for y in range(8):
            spot = (x * 8 + y) * 8
            odd = sums_ref[1024 + spot:1024 + spot + 8, :]
            before = sums_ref[1024 + spot - 8:1024 + spot, :] if y else jnp.zeros((8, 128), f32)
            cross = pltpu.roll(jnp.where(lane < 64, odd, before), 64, 1)
            fine_ref[:, spot * 16:spot * 16 + 128] = sums_ref[spot:spot + 8, :] + cross


def fine_deposit(header, arrived):
    vmem = pl.BlockSpec(memory_space=pltpu.VMEM)
    return pl.pallas_call(
        fine_kernel,
        out_shape=jax.ShapeDtypeStruct((BPH, 16384), f32),
        in_specs=[vmem, vmem],
        out_specs=vmem,
        scratch_shapes=[
            pltpu.VMEM((ROWS, 256), bf16),
            pltpu.VMEM((2048, 128), f32),
            pltpu.VMEM((MB, ROWS), bf16),
        ],
        compiler_params=pltpu.CompilerParams(vmem_limit_bytes=HALF_VMEM),
        cost_estimate=pl.CostEstimate(flops=2 * 2048 * ROWS * 256, bytes_accessed=4000000, transcendentals=0),
        name="fine_deposit",
    )(header, arrived)


def lattice_kernel(
    owner_ref, place_ref, base_ref, blocks_ref, got_ref, out_ref, held_ref, block_ref, got_sem, in_sem, out_sem
):
    copies = [pltpu.make_async_copy(got_ref.at[owner_ref[n]], held_ref.at[n], got_sem.at[n]) for n in range(BPH)]
    copies.append(pltpu.make_async_copy(blocks_ref, block_ref, in_sem.at[0]))
    for copy in copies:
        copy.start()
    firsts = []
    for n in range(BPH):
        first = jnp.int32(n)
        for k in reversed(range(n)):
            first = jnp.where(place_ref[k] >> 2 == place_ref[n] >> 2, k, first)
        firsts.append(first)
    for copy in copies:
        copy.wait()
    quarter = iota((8, 128), 1) // 32
    for n in range(BPH):
        spot = place_ref[n] & 3
        for x in range(CX):
            value = held_ref[n, (x // 4) * 8:(x // 4) * 8 + 8, :]
            moved = pltpu.roll(value, ((spot - x % 4 + 4) & 3) * 32, 1)
            block_ref[firsts[n], x] += jnp.where(quarter == spot, moved, 0.0)
    for n in range(BPH):
        @pl.when(firsts[n] == n)
        def _():
            pltpu.make_async_copy(block_ref.at[n], box_spot(place_ref[n], out_ref), out_sem.at[n]).start()
    for n in range(BPH):
        @pl.when(firsts[n] == n)
        def _():
            pltpu.make_async_copy(block_ref.at[n], box_spot(place_ref[n], out_ref), out_sem.at[n]).wait()


def lattice_add(owners, places, base, blocks, arrived):
    smem = pl.BlockSpec(memory_space=pltpu.SMEM)
    hbm = pl.BlockSpec(memory_space=pltpu.HBM)
    return pl.pallas_call(
        lattice_kernel,
        out_shape=jax.ShapeDtypeStruct((CX, CY, NZ), f32),
        in_specs=[smem, smem, hbm, hbm, hbm],
        out_specs=hbm,
        input_output_aliases={2: 0},
        scratch_shapes=[
            pltpu.VMEM((BPH, 16, 128), f32),
            pltpu.VMEM((BPH, CX, 8, 128), f32),
            pltpu.SemaphoreType.DMA((BPH,)),
            pltpu.SemaphoreType.DMA((1,)),
            pltpu.SemaphoreType.DMA((BPH,)),
        ],
        compiler_params=pltpu.CompilerParams(vmem_limit_bytes=ALL_VMEM),
        cost_estimate=pl.CostEstimate(flops=1000000, bytes_accessed=1000000, transcendentals=0),
        name="lattice_add",
    )(owners, places, base, blocks, arrived)


def shards(
    base_column,
    base_zbin,
    base_frac,
    base_weight,
    fine_column,
    fine_zbin,
    fine_frac,
    fine_weight,
    tile_box,
    box_home,
    box_anchor,
):
    myself = lax.axis_index(AXES).astype(i32)
    homes = lax.dynamic_slice_in_dim(box_home, myself * BPH, BPH, 0)
    outgoing = fine_profiles(tile_box, fine_column, fine_zbin, fine_frac, fine_weight)
    outgoing, base_column, myself = lax.optimization_barrier((outgoing, base_column, myself))
    arrived = lax.all_to_all(outgoing, AXES, split_axis=0, concat_axis=0, tiled=True)
    owners, places = tables(myself.reshape(1), box_home, box_anchor)
    core, front, side, corner = base_deposit(base_column, base_zbin, base_frac, base_weight)
    outer = (shifted(front, "blk", 1), shifted(side, "cross", 1), diagonal(corner))
    arrived, core, owners, places = lax.optimization_barrier((arrived, core, owners, places))
    sending, header = coarse_deposit(homes, arrived)
    sending, header, front, side, corner = lax.optimization_barrier((sending, header, *outer))
    returned = lax.all_to_all(sending, AXES, split_axis=0, concat_axis=0, tiled=True)
    fine_rows = fine_deposit(header, arrived)
    base, blocks = halo_add(places, core, front, side, corner)
    returned, base, blocks, fine_rows = lax.optimization_barrier((returned, base, blocks, fine_rows))
    base_out = lattice_add(owners, places, base, blocks, returned)
    return (base_out, fine_rows)


def solution(mesh):
    placed = (
        P(("blk", "cross")),
        P(("blk", "cross"), None),
        P(None, ("blk", "cross"), None),
        P(("blk", "cross"), None),
        P(("blk", "cross")),
        P(("blk", "cross"), None),
        P(None, ("blk", "cross"), None),
        P(("blk", "cross"), None),
        P(("blk", "cross")),
        P(),
        P(),
    )
    return jax.shard_map(
        shards,
        mesh=mesh,
        in_specs=placed,
        out_specs=(P("blk", "cross", None), P(("blk", "cross"), None)),
        check_vma=False,
    )
```
